32 devices in a mesh: rep: 4 (over y, core), grid: 8 (over z, x).
Axes of the slice: x: 2, y: 2, z: 4, core: 2. Of those that a mesh axis runs over, the one named last changes fastest.
Arguments:
- orbitals: bfloat16 [512, 256], P('rep'), may hold values from -6 to 6
- tiles: bfloat16 [4, 8, 6, 64, 4096], P('rep', 'grid'), may hold values from -0.75 to 0.75
- tile_block: int32 [4, 8, 6], P('rep', 'grid'), may hold values from 0 to 7, as said below
- tile_count: int32 [4, 8], P('rep', 'grid'), may hold values from 1 to 6, as said below
Outputs:
- exchange_action: float32 [512, 256], P('grid')
The draws below stay inside these ranges and needn't reach their ends.
Inputs may be any that keep to these rules, and one draw needn't show every extreme that they name: `tile_block`: the live and empty slots of one (r, g) name distinct basis blocks. Slots at or after tile_count take no part.
All inputs are finite; a program needn't handle non-finite values.
Results may differ from the reference program's by a relative error of at most 0.00061.
Values may be sent and summed in bfloat16 or wider, within the bound.
No kernel may reach another device: no remote copies, remote signals or barrier semaphores. Data moves between devices by JAX's collectives and lax.ppermute only.
A program may use at most 64 MiB of HBM per device.

```python
import math
import jax
import jax.numpy as jnp
from jax import lax

TILE = 64
NORB = 256
CAPT = 6
NBLK = 8
NBAS = 512
N_REP = 4
N_GRID = 8


def draw_tile_block(key, part):
    key = jax.random.fold_in(key, 11)
    row_keys = jax.random.split(key, N_REP * N_GRID)

    def one_row(sub_key):
        return jax.random.permutation(sub_key, NBLK)[:CAPT]
    return jax.vmap(one_row)(row_keys).astype(jnp.int32).reshape(N_REP, N_GRID, CAPT)


def draw_tile_count(key, part):
    key = jax.random.fold_in(key, 23)
    key_base, key_full, key_pick = jax.random.split(key, 3)
    total_rows = N_REP * N_GRID
    base_count = jax.random.randint(key_base, (total_rows,), 1, CAPT // 2 + 1)
    full_flag = jax.random.randint(key_full, (total_rows,), 0, 8) == 0
    chosen = jax.random.randint(key_pick, (), 0, total_rows)
    counts = jnp.where(full_flag, CAPT, base_count)
    counts = jnp.where(jnp.arange(total_rows) == chosen, CAPT, counts)
    return counts.astype(jnp.int32).reshape(N_REP, N_GRID)


def steps_of(own_key, extent, cuts, low, top_value):
    level = 1.0
    for axis_at, parts in cuts:
        heights = jax.random.uniform(jax.random.fold_in(jax.random.fold_in(own_key, 6), axis_at), (parts,), jnp.float32, low / len(cuts), top_value / len(cuts))
        level = level * jnp.repeat(jnp.exp(heights), extent[axis_at] // parts).reshape((-1,) + (1,) * (len(extent) - 1 - axis_at))
    return level


def noise(stream_key, extent, scale, most, cuts=(), kind=jnp.bfloat16):
    entries = jax.random.normal(stream_key, extent, jnp.float32) * scale
    if len(cuts) > 0:
        entries = steps_of(stream_key, extent, cuts, -0.22, 0.18) * entries
    return jnp.clip(entries, min=-most, max=most).astype(kind)


def setup_inputs(seed: int = 0) -> dict:
    seeds = jax.random.split(jax.random.key(seed), 5)
    orbitals = noise(seeds[0], (NBAS, NORB), 1.0, 6.0, ((0, 4),))
    tiles = noise(seeds[1], (N_REP, N_GRID, CAPT, TILE, TILE * TILE), TILE ** -0.5, 0.75, ((0, 4), (1, 8)))
    tile_block = draw_tile_block(jax.random.fold_in(seeds[4], 71), 0)
    tile_count = draw_tile_count(jax.random.fold_in(seeds[4], 71), 0)
    return {"orbitals": orbitals, "tiles": tiles, "tile_block": tile_block, "tile_count": tile_count}


def reference(orbitals, tiles, tile_block, tile_count):
    basis_rows = TILE * N_GRID
    fit_scale = 1.0 / math.sqrt(basis_rows)
    mix_scale = 0.25 / math.sqrt(TILE * N_REP * NORB)
    orbital_f32 = orbitals.astype(jnp.float32)
    blocks = orbital_f32.reshape(N_GRID, TILE, NORB)
    slot_ids = jnp.arange(CAPT, dtype=jnp.int32)

    def one_device(device_args):
        dev_tiles, dev_block, dev_count = device_args
        picked = blocks[dev_block.astype(jnp.int32)]
        live_mask = (slot_ids < dev_count).astype(jnp.float32)
        picked = picked * live_mask[:, None, None]
        product = jnp.einsum('tvk,tvj->kj', dev_tiles.astype(jnp.float32), picked, precision=lax.Precision.HIGHEST)
        return product.astype(jnp.bfloat16)

    def one_rep(rep_args):
        rep_tiles, rep_block, rep_count = rep_args
        intermed = lax.map(one_device, (rep_tiles, rep_block, rep_count))
        intermed = lax.optimization_barrier(intermed.reshape(basis_rows, TILE * NORB))
        intermed = intermed.astype(jnp.float32)
        fitted = fit_scale * jnp.dot(intermed.T, orbital_f32, precision=lax.Precision.HIGHEST)
        fitted = lax.optimization_barrier(fitted.astype(jnp.bfloat16)).astype(jnp.float32)
        return jnp.dot(intermed, fitted, precision=lax.Precision.HIGHEST)
    per_rep = lax.map(one_rep, (tiles, tile_block, tile_count))
    return -mix_scale * lax.optimization_barrier(jnp.sum(per_rep, axis=0))
```

```python
import functools
import math

import jax
import jax.numpy as jnp
from jax import lax
from jax.experimental import pallas as pl
from jax.experimental.pallas import tpu as pltpu
from jax.sharding import PartitionSpec as P

LANES = 128
SUB = 16


def contract_kernel(count_ref, block_ref, orb_ref, swap_ref, tiles_ref, out_ref, buf, picked, sems):
    slots, width, extent = tiles_ref.shape
    norb = orb_ref.shape[1]
    half = norb // 2
    parts = out_ref.shape[0]
    per_part = half // parts
    step = SUB * width
    chunks = extent // step

    def copy(at):
        lanes = pl.ds(at * step, step)
        return pltpu.make_async_copy(tiles_ref.at[:, :, lanes], buf.at[:, :, lanes], sems.at[at])

    for at in range(chunks):
        copy(at).start()
    for t in range(slots):
        row = pl.multiple_of(block_ref[0, 0, t] * width, width)
        rows = orb_ref[pl.ds(row, width), :]
        picked[t * width:(t + 1) * width, :] = jnp.where(t < count_ref[0, 0], rows, jnp.zeros_like(rows))
    lhs = picked[...].T
    swap = swap_ref[...]
    low = lax.broadcasted_iota(jnp.int32, (half, LANES), 1) < width
    for at in range(chunks):
        copy(at).wait()
        lanes = slice(at * step, (at + 1) * step)
        rhs = buf[:, :, lanes].reshape(slots * width, step)
        acc = jnp.dot(lhs, rhs, preferred_element_type=jnp.float32)
        per_mu = []
        for q in range(step // LANES):
            a = acc[:half, q * LANES:(q + 1) * LANES]
            b = acc[half:, q * LANES:(q + 1) * LANES]
            per_mu.append(jnp.where(low, a, pltpu.roll(b, width, 1)).astype(jnp.bfloat16))
            per_mu.append(jnp.where(low, pltpu.roll(a, width, 1), b).astype(jnp.bfloat16))
        for s in range(half // (2 * SUB)):
            r0 = 2 * s * SUB
            left = jnp.concatenate([m[r0:r0 + SUB] for m in per_mu], axis=0)
            right = jnp.concatenate([m[r0 + SUB:r0 + 2 * SUB] for m in per_mu], axis=0)
            moved = jnp.dot(swap, jnp.concatenate([left, right], axis=1), preferred_element_type=jnp.float32)
            moved = moved.astype(jnp.bfloat16)
            for side in range(2):
                for k in range(SUB):
                    i_lo = r0 + side * SUB + k
                    h, l = divmod(i_lo, per_part)
                    out_ref[h, at * SUB:(at + 1) * SUB, l * LANES:(l + 1) * LANES] = moved[
                        k * SUB:(k + 1) * SUB, side * LANES:(side + 1) * LANES
                    ]


def contract(count, block, orbitals, tiles, parts):
    slots, width, extent = tiles.shape
    norb = orbitals.shape[1]
    pos = jnp.arange(SUB * SUB, dtype=jnp.int32)
    swap = (pos[None, :] == ((pos % SUB) * SUB + pos // SUB)[:, None]).astype(jnp.bfloat16)
    cols = width * norb // parts
    return pl.pallas_call(
        contract_kernel,
        out_shape=jax.ShapeDtypeStruct((parts, width, cols), jnp.bfloat16),
        in_specs=[
            pl.BlockSpec(memory_space=pltpu.SMEM),
            pl.BlockSpec(memory_space=pltpu.SMEM),
            pl.BlockSpec(memory_space=pltpu.VMEM),
            pl.BlockSpec(memory_space=pltpu.VMEM),
            pl.BlockSpec(memory_space=pl.ANY),
        ],
        out_specs=pl.BlockSpec(memory_space=pltpu.VMEM),
        scratch_shapes=[
            pltpu.VMEM((slots, width, extent), jnp.bfloat16),
            pltpu.VMEM((slots * width, norb), jnp.bfloat16),
            pltpu.SemaphoreType.DMA((extent // (SUB * width),)),
        ],
        compiler_params=pltpu.CompilerParams(vmem_limit_bytes=32 * 1024 * 1024),
        cost_estimate=pl.CostEstimate(
            flops=2 * slots * width * extent * norb, bytes_accessed=2 * slots * width * extent, transcendentals=0
        ),
    )(count, block, orbitals, swap, tiles)


def action_kernel(fit_scale, mix_scale, step, orb_ref, rows_ref, out_ref):
    orb_t = orb_ref[...].T
    for at in range(rows_ref.shape[1] // step):
        part = rows_ref[:, at * step:(at + 1) * step]
        fitted = (fit_scale * jnp.dot(orb_t, part, preferred_element_type=jnp.float32)).astype(jnp.bfloat16)
        term = lax.dot_general(part, fitted, (((1,), (1,)), ((), ())), preferred_element_type=jnp.float32)
        term = -mix_scale * term
        if at == 0:
            out_ref[...] = term
        else:
            out_ref[...] += term


def action(orbitals, rows, fit_scale, mix_scale):
    step = min(512, rows.shape[1])
    return pl.pallas_call(
        functools.partial(action_kernel, fit_scale, mix_scale, step),
        out_shape=jax.ShapeDtypeStruct(orbitals.shape, jnp.float32),
        in_specs=[pl.BlockSpec(memory_space=pltpu.VMEM)] * 2,
        out_specs=pl.BlockSpec(memory_space=pltpu.VMEM),
        compiler_params=pltpu.CompilerParams(vmem_limit_bytes=32 * 1024 * 1024),
        cost_estimate=pl.CostEstimate(
            flops=4 * rows.shape[0] * rows.shape[1] * orbitals.shape[1],
            bytes_accessed=2 * rows.shape[0] * rows.shape[1],
            transcendentals=0,
        ),
    )(orbitals, rows)


def per_device(orbitals, tiles, tile_block, tile_count):
    rep_size = lax.axis_size("rep")
    grid_size = lax.axis_size("grid")
    width = tiles.shape[3]
    norb = orbitals.shape[1]
    full = lax.all_gather(orbitals, "rep", axis=0, tiled=True)
    basis_rows = full.shape[0]
    fit_scale = 1.0 / math.sqrt(basis_rows)
    mix_scale = 0.25 / math.sqrt(width * rep_size * norb)
    local = contract(tile_count, tile_block, full, tiles[0, 0], grid_size)
    received = lax.all_to_all(local, "grid", split_axis=0, concat_axis=0, tiled=True)
    part = action(full, received.reshape(basis_rows, -1), fit_scale, mix_scale)
    shares = lax.all_to_all(part.reshape(grid_size, width, norb), "grid", split_axis=0, concat_axis=0, tiled=True)
    mine = jnp.sum(shares, axis=0)
    every = lax.all_gather(mine, "rep", axis=0, tiled=False)
    return jnp.sum(every, axis=0)


def solution(mesh):
    in_specs = (
        P("rep", None),
        P("rep", "grid", None, None, None),
        P("rep", "grid", None),
        P("rep", "grid"),
    )
    return jax.shard_map(
        per_device, mesh=mesh, in_specs=in_specs, out_specs=P("grid", None), check_vma=False
    )
```

```python
import functools
import math

import jax
import jax.numpy as jnp
from jax import lax
from jax.experimental import pallas as pl
from jax.experimental.pallas import tpu as pltpu
from jax.sharding import PartitionSpec as P

LANES = 128
SUB = 16
VMEM_LIMIT = 24 * 1024 * 1024


def contract_kernel(group_starts, place, skip, count, block_hbm, orb_ref, tiles_hbm, *refs):
    outs, (buf, picked, turned, block, sems, block_sem) = refs[skip:-6], refs[-6:]
    slots, width, extent = tiles_hbm.shape[2:]
    half = orb_ref.shape[1] // 2
    step = SUB * width
    chunks = extent // step


    def copy(at):
        lanes = pl.ds(at * step, step)
        return pltpu.make_async_copy(tiles_hbm.at[0, 0, :, :, lanes], buf.at[:, :, lanes], sems.at[at])

    block_copy = pltpu.make_async_copy(block_hbm, block, block_sem.at[0])
    block_copy.start()
    for at in range(chunks):
        copy(at).start()
    row_at = lax.broadcasted_iota(jnp.int32, (SUB * SUB, SUB * SUB), 0)
    col_at = lax.broadcasted_iota(jnp.int32, (SUB * SUB, SUB * SUB), 1)
    swap = (col_at == (row_at % SUB) * SUB + row_at // SUB).astype(jnp.bfloat16)
    low = lax.broadcasted_iota(jnp.int32, (SUB, LANES), 1) < width
    block_copy.wait()
    for t in range(slots):
        row = pl.multiple_of(block[0, 0, t] * width, width)
        rows = orb_ref[pl.ds(row, width), :]
        picked[t * width:(t + 1) * width, :] = jnp.where(t < count[0, 0], rows, jnp.zeros_like(rows))
    turned[...] = picked[...].T
    starts = group_starts()
    groups = len(starts)
    lhs = jnp.concatenate(
        [turned[pl.ds(pl.multiple_of(at, SUB), SUB), :] for at in starts]
        + [turned[pl.ds(pl.multiple_of(half + at, SUB), SUB), :] for at in starts],
        axis=0,
    )
    for at in range(chunks):
        copy(at).wait()
        rhs = buf[:, :, at * step:(at + 1) * step].reshape(slots * width, step)
        acc = jnp.dot(lhs, rhs, preferred_element_type=jnp.float32)
        for s in range(0, groups, 2):
            sides = []
            for g in (s, s + 1):
                per_mu = []
                for q in range(step // LANES):
                    a = acc[g * SUB:(g + 1) * SUB, q * LANES:(q + 1) * LANES]
                    b = acc[(groups + g) * SUB:(groups + g + 1) * SUB, q * LANES:(q + 1) * LANES]
                    per_mu.append(jnp.where(low, a, pltpu.roll(b, width, 1)).astype(jnp.bfloat16))
                    per_mu.append(jnp.where(low, pltpu.roll(a, width, 1), b).astype(jnp.bfloat16))
                sides.append(jnp.concatenate(per_mu, axis=0))
            moved = jnp.dot(swap, jnp.concatenate(sides, axis=1), preferred_element_type=jnp.float32)
            moved = moved.astype(jnp.bfloat16)
            for side in range(2):
                for k in range(SUB):
                    which, part, col = place(s + side, k)
                    outs[which][part, at * SUB:(at + 1) * SUB, col * LANES:(col + 1) * LANES] = moved[
                        k * SUB:(k + 1) * SUB, side * LANES:(side + 1) * LANES
                    ]


def in_hbm(x):
    return pltpu.with_memory_space_constraint(x, pltpu.HBM)


def contract(group_starts, place, out_shapes, count, block, orbitals, tiles, after=None):
    later = [] if after is None else [after]
    slots, width, extent = tiles.shape[2:]
    norb = orbitals.shape[1]
    made = sum(math.prod(shape) for shape in out_shapes)
    return pl.pallas_call(
        functools.partial(contract_kernel, group_starts, place, len(later)),
        out_shape=[jax.ShapeDtypeStruct(shape, jnp.bfloat16) for shape in out_shapes],
        in_specs=[
            pl.BlockSpec(memory_space=pltpu.SMEM),
            pl.BlockSpec(memory_space=pltpu.HBM),
            pl.BlockSpec(memory_space=pltpu.VMEM),
            pl.BlockSpec(memory_space=pltpu.HBM),
        ]
        + [pl.BlockSpec(memory_space=pl.ANY)] * len(later),
        out_specs=[pl.BlockSpec(memory_space=pltpu.VMEM)] * len(out_shapes),
        scratch_shapes=[
            pltpu.VMEM((slots, width, extent), jnp.bfloat16),
            pltpu.VMEM((slots * width, norb), jnp.bfloat16),
            pltpu.VMEM((norb, slots * width), jnp.bfloat16),
            pltpu.SMEM(block.shape, jnp.int32),
            pltpu.SemaphoreType.DMA((extent // (SUB * width),)),
            pltpu.SemaphoreType.DMA((1,)),
        ],
        compiler_params=pltpu.CompilerParams(vmem_limit_bytes=VMEM_LIMIT),
        cost_estimate=pl.CostEstimate(
            flops=2 * slots * width * made, bytes_accessed=2 * slots * width * extent + 2 * made, transcendentals=0
        ),
    )(count, in_hbm(block), orbitals, in_hbm(tiles), *later)


def orbital_rows(orb_ref, width, ids):
    rows = [orb_ref[pl.ds(pl.multiple_of(b * width, width), width), :] for b in ids]
    return jnp.concatenate(rows, axis=0).T


def joined(refs, lanes=slice(None)):
    return jnp.concatenate([ref[:, :, lanes].reshape(-1, ref[:, :, lanes].shape[2]) for ref in refs], axis=0)


def fit_kernel(step, ids, orb_ref, *refs):
    rows, out_ref = refs[:-1], refs[-1]
    turned = orbital_rows(orb_ref, rows[0].shape[1], ids())
    for at in range(out_ref.shape[1] // step):
        lanes = slice(at * step, (at + 1) * step)
        out_ref[:, lanes] = jnp.dot(turned, joined(rows, lanes), preferred_element_type=jnp.float32)


def fit(orbitals, rows, ids):
    width, cols = rows[0].shape[1:]
    number = sum(each.shape[0] for each in rows)
    norb = orbitals.shape[1]
    return pl.pallas_call(
        functools.partial(fit_kernel, min(512, cols), ids),
        out_shape=jax.ShapeDtypeStruct((norb, cols), jnp.float32),
        in_specs=[pl.BlockSpec(memory_space=pltpu.VMEM)] * (1 + len(rows)),
        out_specs=pl.BlockSpec(memory_space=pltpu.VMEM),
        compiler_params=pltpu.CompilerParams(vmem_limit_bytes=VMEM_LIMIT),
        cost_estimate=pl.CostEstimate(
            flops=2 * number * width * cols * norb,
            bytes_accessed=2 * number * width * cols + 4 * norb * cols,
            transcendentals=0,
        ),
    )(orbitals, *rows)


def action_kernel(fit_scale, mix_scale, step, early_ids, late_ids, n_early, fitted_ref, orb_ref, *refs):
    early, late, (keep_ref, send_ref, fitted) = refs[:n_early], refs[n_early:-3], refs[-3:]
    width, cols = early[0].shape[1:]
    norb = orb_ref.shape[1]
    upper = lax.axis_index("rep") % 2 == 1
    if late:
        turned = orbital_rows(orb_ref, width, late_ids())
    for at in range(cols // step):
        lanes = slice(at * step, (at + 1) * step)
        total = fitted_ref[:, lanes]
        if late:
            total = total + jnp.dot(turned, joined(late, lanes), preferred_element_type=jnp.float32)
        fitted[:, lanes] = (fit_scale * total).astype(jnp.bfloat16)
    parts = [(early_ids(), early)]
    if late:
        parts.append((late_ids(), late))
    for ids, rows in parts:
        term = lax.dot_general(joined(rows), fitted[...], (((1,), (1,)), ((), ())), preferred_element_type=jnp.float32)
        term = (-mix_scale * term).reshape(len(ids), 2, width // 2, norb)
        keep = jnp.where(upper, term[:, 1], term[:, 0])
        send = jnp.where(upper, term[:, 0], term[:, 1])
        for k, b in enumerate(ids):
            keep_ref[b] = keep[k]
            send_ref[b] = send[k]


def action(orbitals, fitted, early, late, early_ids, late_ids, fit_scale, mix_scale):
    width, cols = early[0].shape[1:]
    blocks = orbitals.shape[0] // width
    norb = orbitals.shape[1]
    shape = jax.ShapeDtypeStruct((blocks, width // 2, norb), jnp.float32)
    return pl.pallas_call(
        functools.partial(action_kernel, fit_scale, mix_scale, min(512, cols), early_ids, late_ids, len(early)),
        out_shape=[shape, shape],
        in_specs=[pl.BlockSpec(memory_space=pltpu.VMEM)] * (2 + len(early) + len(late)),
        out_specs=[pl.BlockSpec(memory_space=pltpu.VMEM)] * 2,
        scratch_shapes=[pltpu.VMEM((norb, cols), jnp.bfloat16)],
        compiler_params=pltpu.CompilerParams(vmem_limit_bytes=VMEM_LIMIT),
        cost_estimate=pl.CostEstimate(
            flops=4 * blocks * width * cols * norb, bytes_accessed=2 * blocks * width * cols, transcendentals=0
        ),
    )(fitted, orbitals, *early, *late)


def per_device(orbitals, tiles, tile_block, tile_count):
    rep_size = lax.axis_size("rep")
    grid_size = lax.axis_size("grid")
    width = tiles.shape[3]
    norb = orbitals.shape[1]
    half = norb // 2
    cols = width * norb // grid_size
    full = lax.all_gather(orbitals, "rep", axis=0, tiled=True)
    fit_scale = 1.0 / math.sqrt(full.shape[0])
    mix_scale = 0.25 / math.sqrt(width * rep_size * norb)
    args = (tile_count, tile_block, full, tiles)
    per_part = half // grid_size
    if per_part == SUB and grid_size % 4 == 0 and grid_size & (grid_size - 1) == 0:
        near_size = grid_size // 2

        def far_blocks():
            me = lax.axis_index("grid")
            return [me ^ (near_size + k) for k in range(near_size)]

        def near_blocks():
            me = lax.axis_index("grid")
            return [me ^ k for k in range(near_size)]

        sent_far = contract(
            lambda: [b * SUB for b in far_blocks()], lambda s, k: (s, 0, k), [(1, width, cols)] * near_size, *args
        )
        far = [
            lax.ppermute(sent, "grid", [(i, i ^ (near_size + k)) for i in range(grid_size)])
            for k, sent in enumerate(sent_far)
        ]
        sent_near = contract(
            lambda: [b * SUB for b in near_blocks()], lambda s, k: (s, 0, k), [(1, width, cols)] * near_size, *args,
            after=sent_far[0],
        )
        near = [sent_near[0]] + [
            lax.ppermute(sent, "grid", [(i, i ^ k) for i in range(grid_size)])
            for k, sent in enumerate(sent_near) if k
        ]
        early, late, early_ids, late_ids = far, near, far_blocks, near_blocks
    else:
        def place(s, k):
            part, col = divmod(s * SUB + k, per_part)
            return 0, part, col

        (sent,) = contract(
            lambda: list(range(0, half, SUB)), place, [(grid_size, width, cols)], *args
        )
        early, late = [lax.all_to_all(sent, "grid", 0, 0, tiled=True)], []

        def early_ids():
            return list(range(grid_size))

        late_ids = None
    fitted = fit(full, early, early_ids)
    part_keep, part_send = action(full, fitted, early, late, early_ids, late_ids, fit_scale, mix_scale)
    pair = part_keep + lax.ppermute(part_send, "rep", [(i, i ^ 1) for i in range(rep_size)])
    mine = jnp.sum(lax.all_to_all(pair, "grid", 0, 0, tiled=True), axis=0)
    every = lax.all_gather(mine, "rep", axis=0, tiled=False)
    return jnp.sum(every.reshape(rep_size // 2, 2, width // 2, norb), axis=0).reshape(width, norb)


def solution(mesh):
    in_specs = (
        P("rep", None),
        P("rep", "grid", None, None, None),
        P("rep", "grid", None),
        P("rep", "grid"),
    )
    return jax.shard_map(
        per_device, mesh=mesh, in_specs=in_specs, out_specs=P("grid", None), check_vma=False
    )
```

```python
import functools
import math

import jax
import jax.numpy as jnp
from jax import lax
from jax.experimental import pallas as pl
from jax.experimental.pallas import tpu as pltpu
from jax.sharding import PartitionSpec as P

LANES = 128
SUB = 16
VMEM_LIMIT = 24 * 1024 * 1024


def load_kernel(count_ref, block_hbm, tiles_hbm, out_ref, live_ref, block, sems, block_sem):
    chunks = sems.shape[0]
    step = out_ref.shape[2] // chunks
    copies = [
        pltpu.make_async_copy(
            tiles_hbm.at[0, 0, :, :, pl.ds(at * step, step)], out_ref.at[:, :, pl.ds(at * step, step)], sems.at[at]
        )
        for at in range(chunks)
    ]
    block_copy = pltpu.make_async_copy(block_hbm, block, block_sem.at[0])
    block_copy.start()
    for each in copies:
        each.start()
    block_copy.wait()
    slot = lax.broadcasted_iota(jnp.int32, live_ref.shape, 1)
    live_ref[...] = jnp.where(slot < count_ref[0, 0], block[0], -1)
    for each in copies:
        each.wait()


def in_hbm(x):
    return pltpu.with_memory_space_constraint(x, pltpu.HBM)


def load(tiles, count, block):
    return pl.pallas_call(
        load_kernel,
        out_shape=[
            jax.ShapeDtypeStruct(tiles.shape[2:], tiles.dtype),
            jax.ShapeDtypeStruct(block.shape[1:], block.dtype),
        ],
        in_specs=[
            pl.BlockSpec(memory_space=pltpu.SMEM),
            pl.BlockSpec(memory_space=pltpu.HBM),
            pl.BlockSpec(memory_space=pltpu.HBM),
        ],
        out_specs=[pl.BlockSpec(memory_space=pltpu.VMEM)] * 2,
        scratch_shapes=[
            pltpu.VMEM(block.shape, block.dtype),
            pltpu.SemaphoreType.DMA((4,)),
            pltpu.SemaphoreType.DMA((1,)),
        ],
        compiler_params=pltpu.CompilerParams(vmem_limit_bytes=VMEM_LIMIT),
        cost_estimate=pl.CostEstimate(flops=0, bytes_accessed=2 * math.prod(tiles.shape), transcendentals=0),
    )(count, in_hbm(block), in_hbm(tiles))


def multiply(turned_ref, tiles_ref, group_starts, place, outs):
    slots, width, extent = tiles_ref.shape
    half = turned_ref.shape[0] // 2
    step = SUB * width
    row_at = lax.broadcasted_iota(jnp.int32, (SUB * SUB, SUB * SUB), 0)
    col_at = lax.broadcasted_iota(jnp.int32, (SUB * SUB, SUB * SUB), 1)
    bits = SUB.bit_length() - 1
    swap = (col_at == ((row_at & (SUB - 1)) << bits) + (row_at >> bits)).astype(jnp.bfloat16)
    low = lax.broadcasted_iota(jnp.int32, (SUB, LANES), 1) < width
    groups = len(group_starts)
    lhs = jnp.concatenate(
        [
            turned_ref[pl.ds(pl.multiple_of(first + at, SUB), SUB), :]
            for first in (0, half)
            for at in group_starts
        ],
        axis=0,
    )
    chunks = extent // step
    sides = []
    for at in range(chunks):
        rhs = tiles_ref[:, :, at * step:(at + 1) * step].reshape(slots * width, step)
        acc = jnp.dot(lhs, rhs, preferred_element_type=jnp.float32)
        for s in range(groups):
            per_mu = []
            for q in range(step // LANES):
                a = acc[s * SUB:(s + 1) * SUB, q * LANES:(q + 1) * LANES]
                b = acc[(groups + s) * SUB:(groups + s + 1) * SUB, q * LANES:(q + 1) * LANES]
                per_mu.append(jnp.where(low, a, pltpu.roll(b, width, 1)).astype(jnp.bfloat16))
                per_mu.append(jnp.where(low, pltpu.roll(a, width, 1), b).astype(jnp.bfloat16))
            sides.append((at, s, jnp.concatenate(per_mu, axis=0)))
    moved = jnp.dot(
        swap, jnp.concatenate([side for _, _, side in sides], axis=1), preferred_element_type=jnp.float32
    ).astype(jnp.bfloat16)
    for n, (at, s, _) in enumerate(sides):
        for k in range(SUB):
            which, part, col = place(s, k)
            outs[which][part, at * SUB:(at + 1) * SUB, col * LANES:(col + 1) * LANES] = moved[
                k * SUB:(k + 1) * SUB, n * LANES:(n + 1) * LANES
            ]


def first_kernel(group_starts, place, n_parts, block_ref, tiles_ref, *refs):
    parts, (full_ref, turned_ref, *outs), picked = refs[:n_parts], refs[n_parts:-1], refs[-1]
    slots, width, _ = tiles_ref.shape
    depth = parts[0].shape[0]
    me = lax.axis_index("rep") if n_parts > 1 else 0
    for k in range(n_parts):
        full_ref[pl.ds(pl.multiple_of((me ^ k) * depth, depth), depth), :] = parts[k][...]
    for t in range(slots):
        row = pl.multiple_of(jnp.maximum(block_ref[0, t], 0) * width, width)
        rows = full_ref[pl.ds(row, width), :]
        picked[t * width:(t + 1) * width, :] = jnp.where(block_ref[0, t] >= 0, rows, jnp.zeros_like(rows))
    turned_ref[...] = picked[...].T
    multiply(turned_ref, tiles_ref, group_starts(), place, outs)


def next_kernel(group_starts, place, turned_ref, tiles_ref, skipped, *outs):
    multiply(turned_ref, tiles_ref, group_starts(), place, outs)


def contract_cost(tiles, norb, out_shapes):
    slots, width, extent = tiles.shape
    made = sum(math.prod(shape) for shape in out_shapes)
    return pl.CostEstimate(
        flops=2 * slots * width * made, bytes_accessed=2 * slots * width * extent + 2 * made, transcendentals=0
    )


def contract_first(group_starts, place, out_shapes, block, tiles, parts):
    slots, width, _ = tiles.shape
    depth, norb = parts[0].shape
    shapes = [(depth * len(parts), norb), (norb, slots * width)] + out_shapes
    full, turned, *made = pl.pallas_call(
        functools.partial(first_kernel, group_starts, place, len(parts)),
        out_shape=[jax.ShapeDtypeStruct(shape, jnp.bfloat16) for shape in shapes],
        in_specs=[pl.BlockSpec(memory_space=pltpu.SMEM)]
        + [pl.BlockSpec(memory_space=pltpu.VMEM)] * (1 + len(parts)),
        out_specs=[pl.BlockSpec(memory_space=pltpu.VMEM)] * len(shapes),
        scratch_shapes=[pltpu.VMEM((slots * width, norb), jnp.bfloat16)],
        compiler_params=pltpu.CompilerParams(vmem_limit_bytes=VMEM_LIMIT),
        cost_estimate=contract_cost(tiles, norb, out_shapes),
    )(block, tiles, *parts)
    return full, turned, made


def contract_next(group_starts, place, out_shapes, turned, tiles, after):
    return pl.pallas_call(
        functools.partial(next_kernel, group_starts, place),
        out_shape=[jax.ShapeDtypeStruct(shape, jnp.bfloat16) for shape in out_shapes],
        in_specs=[pl.BlockSpec(memory_space=pltpu.VMEM)] * 2 + [pl.BlockSpec(memory_space=pl.ANY)],
        out_specs=[pl.BlockSpec(memory_space=pltpu.VMEM)] * len(out_shapes),
        compiler_params=pltpu.CompilerParams(vmem_limit_bytes=VMEM_LIMIT),
        cost_estimate=contract_cost(tiles, turned.shape[0], out_shapes),
    )(turned, tiles, after)


def orbital_rows(orb_ref, width, ids):
    rows = [orb_ref[pl.ds(pl.multiple_of(b * width, width), width), :] for b in ids]
    return jnp.concatenate(rows, axis=0).T


def joined(refs, lanes=slice(None)):
    return jnp.concatenate([ref[:, :, lanes].reshape(-1, ref[:, :, lanes].shape[2]) for ref in refs], axis=0)


def fit_kernel(step, ids, orb_ref, *refs):
    rows, out_ref = refs[:-1], refs[-1]
    turned = orbital_rows(orb_ref, rows[0].shape[1], ids())
    for at in range(out_ref.shape[1] // step):
        lanes = slice(at * step, (at + 1) * step)
        out_ref[:, lanes] = jnp.dot(turned, joined(rows, lanes), preferred_element_type=jnp.float32)


def fit(orbitals, rows, ids):
    width, cols = rows[0].shape[1:]
    number = sum(each.shape[0] for each in rows)
    norb = orbitals.shape[1]
    return pl.pallas_call(
        functools.partial(fit_kernel, min(512, cols), ids),
        out_shape=jax.ShapeDtypeStruct((norb, cols), jnp.float32),
        in_specs=[pl.BlockSpec(memory_space=pltpu.VMEM)] * (1 + len(rows)),
        out_specs=pl.BlockSpec(memory_space=pltpu.VMEM),
        compiler_params=pltpu.CompilerParams(vmem_limit_bytes=VMEM_LIMIT),
        cost_estimate=pl.CostEstimate(
            flops=2 * number * width * cols * norb,
            bytes_accessed=2 * number * width * cols + 4 * norb * cols,
            transcendentals=0,
        ),
    )(orbitals, *rows)


def action_kernel(fit_scale, mix_scale, step, early_ids, late_ids, n_early, fitted_ref, orb_ref, *refs):
    early, late, (keep_ref, send_ref, fitted) = refs[:n_early], refs[n_early:-3], refs[-3:]
    width, cols = early[0].shape[1:]
    norb = orb_ref.shape[1]
    upper = lax.axis_index("rep") % 2 == 1
    if late:
        turned = orbital_rows(orb_ref, width, late_ids())
    for at in range(cols // step):
        lanes = slice(at * step, (at + 1) * step)
        total = fitted_ref[:, lanes]
        if late:
            total = total + jnp.dot(turned, joined(late, lanes), preferred_element_type=jnp.float32)
        fitted[:, lanes] = (fit_scale * total).astype(jnp.bfloat16)
    parts = [(early_ids(), early)]
    if late:
        parts.append((late_ids(), late))
    for ids, rows in parts:
        term = lax.dot_general(joined(rows), fitted[...], (((1,), (1,)), ((), ())), preferred_element_type=jnp.float32)
        term = (-mix_scale * term).reshape(len(ids), 2, width // 2, norb)
        keep = jnp.where(upper, term[:, 1], term[:, 0])
        send = jnp.where(upper, term[:, 0], term[:, 1])
        for k, b in enumerate(ids):
            keep_ref[b] = keep[k]
            send_ref[b] = send[k]


def action(orbitals, fitted, early, late, early_ids, late_ids, fit_scale, mix_scale):
    width, cols = early[0].shape[1:]
    blocks = orbitals.shape[0] // width
    norb = orbitals.shape[1]
    shape = jax.ShapeDtypeStruct((blocks, width // 2, norb), jnp.float32)
    return pl.pallas_call(
        functools.partial(action_kernel, fit_scale, mix_scale, min(512, cols), early_ids, late_ids, len(early)),
        out_shape=[shape, shape],
        in_specs=[pl.BlockSpec(memory_space=pltpu.VMEM)] * (2 + len(early) + len(late)),
        out_specs=[pl.BlockSpec(memory_space=pltpu.VMEM)] * 2,
        scratch_shapes=[pltpu.VMEM((norb, cols), jnp.bfloat16)],
        compiler_params=pltpu.CompilerParams(vmem_limit_bytes=VMEM_LIMIT),
        cost_estimate=pl.CostEstimate(
            flops=4 * blocks * width * cols * norb, bytes_accessed=2 * blocks * width * cols, transcendentals=0
        ),
    )(fitted, orbitals, *early, *late)


def swapped(x, axis, k):
    return lax.ppermute(x, axis, [(i, i ^ k) for i in range(lax.axis_size(axis))])


def per_device(orbitals, tiles, tile_block, tile_count):
    rep_size = lax.axis_size("rep")
    grid_size = lax.axis_size("grid")
    width = tiles.shape[3]
    depth, norb = orbitals.shape
    half = norb // 2
    cols = width * norb // grid_size
    basis_rows = depth * rep_size
    fit_scale = 1.0 / math.sqrt(basis_rows)
    mix_scale = 0.25 / math.sqrt(width * rep_size * norb)
    inside, block = load(tiles, tile_count, tile_block)
    per_part = half // grid_size
    if per_part == SUB and grid_size == 8 and rep_size == 4:
        near_size = grid_size // 2
        parts = [orbitals] + [swapped(orbitals, "rep", k) for k in range(1, rep_size)]

        def ids(ks):
            def blocks():
                me = lax.axis_index("grid")
                return [me ^ k for k in ks]

            return blocks

        def starts(ks):
            return lambda: [b * SUB for b in ids(ks)()]

        def own_output(s, k):
            return s, 0, k

        def shapes(ks):
            return [(1, width, cols)] * len(ks)

        waves, late_ks = [[4], [0, 1, 2, 3], [5, 6, 7]], [5, 6, 7]
        full, turned, made = contract_first(
            starts(waves[0]), own_output, shapes(waves[0]), block, inside, parts
        )
        sent = dict(zip(waves[0], made))
        for wave in waves[1:]:
            made = contract_next(starts(wave), own_output, shapes(wave), turned, inside, made[0])
            sent.update(zip(wave, made))
        received = {k: swapped(sent[k], "grid", k) if k else sent[k] for wave in waves for k in wave}
        early_ks = [k for wave in waves for k in wave if k not in late_ks]
        early, late = [received[k] for k in early_ks], [received[k] for k in late_ks]
        early_ids, late_ids = ids(early_ks), ids(late_ks)
    else:
        def place(s, k):
            part, col = divmod(s * SUB + k, per_part)
            return 0, part, col

        parts = [lax.all_gather(orbitals, "rep", axis=0, tiled=True)]
        full, _, (sent,) = contract_first(
            lambda: list(range(0, half, SUB)), place, [(grid_size, width, cols)], block, inside, parts
        )
        early, late = [lax.all_to_all(sent, "grid", 0, 0, tiled=True)], []

        def early_ids():
            return list(range(grid_size))

        late_ids = None
    fitted = fit(full, early, early_ids)
    part_keep, part_send = action(full, fitted, early, late, early_ids, late_ids, fit_scale, mix_scale)
    pair = part_keep + swapped(part_send, "rep", 1)
    mine = jnp.sum(lax.all_to_all(pair, "grid", 0, 0, tiled=True), axis=0)
    if rep_size == 4:
        other, across = swapped(mine, "rep", 2), swapped(mine, "rep", 3)
        beside = swapped(mine, "rep", 1)
        own, theirs = mine + other, beside + across
        upper = lax.axis_index("rep") % 2 == 1
        return jnp.concatenate([jnp.where(upper, theirs, own), jnp.where(upper, own, theirs)], axis=0)
    every = lax.all_gather(mine, "rep", axis=0, tiled=False)
    return jnp.sum(every.reshape(rep_size // 2, 2, width // 2, norb), axis=0).reshape(width, norb)


def solution(mesh):
    in_specs = (
        P("rep", None),
        P("rep", "grid", None, None, None),
        P("rep", "grid", None),
        P("rep", "grid"),
    )
    return jax.shard_map(
        per_device, mesh=mesh, in_specs=in_specs, out_specs=P("grid", None), check_vma=False
    )
```

```python
import functools
import math

import jax
import jax.numpy as jnp
from jax import lax
from jax.experimental import pallas as pl
from jax.experimental.pallas import tpu as pltpu
from jax.sharding import PartitionSpec as P

LANES = 128
SUB = 16
VMEM_LIMIT = 24 * 1024 * 1024


def load_kernel(count_ref, block_hbm, tiles_hbm, out_ref, live_ref, block, sems, block_sem):
    chunks = sems.shape[0]
    step = out_ref.shape[2] // chunks
    copies = [
        pltpu.make_async_copy(
            tiles_hbm.at[0, 0, :, :, pl.ds(at * step, step)], out_ref.at[:, :, pl.ds(at * step, step)], sems.at[at]
        )
        for at in range(chunks)
    ]
    block_copy = pltpu.make_async_copy(block_hbm, block, block_sem.at[0])
    block_copy.start()
    for each in copies:
        each.start()
    block_copy.wait()
    slot = lax.broadcasted_iota(jnp.int32, live_ref.shape, 1)
    live_ref[...] = jnp.where(slot < count_ref[0, 0], block[0], -1)
    for each in copies:
        each.wait()


def in_hbm(x):
    return pltpu.with_memory_space_constraint(x, pltpu.HBM)


def load(tiles, count, block):
    return pl.pallas_call(
        load_kernel,
        out_shape=[
            jax.ShapeDtypeStruct(tiles.shape[2:], tiles.dtype),
            jax.ShapeDtypeStruct(block.shape[1:], block.dtype),
        ],
        in_specs=[
            pl.BlockSpec(memory_space=pltpu.SMEM),
            pl.BlockSpec(memory_space=pltpu.HBM),
            pl.BlockSpec(memory_space=pltpu.HBM),
        ],
        out_specs=[pl.BlockSpec(memory_space=pltpu.VMEM)] * 2,
        scratch_shapes=[
            pltpu.VMEM(block.shape, block.dtype),
            pltpu.SemaphoreType.DMA((4,)),
            pltpu.SemaphoreType.DMA((1,)),
        ],
        compiler_params=pltpu.CompilerParams(vmem_limit_bytes=VMEM_LIMIT),
        cost_estimate=pl.CostEstimate(flops=0, bytes_accessed=2 * math.prod(tiles.shape), transcendentals=0),
    )(count, in_hbm(block), in_hbm(tiles))


def multiply(turned_ref, tiles_ref, group_starts, place, outs):
    slots, width, extent = tiles_ref.shape
    half = turned_ref.shape[0] // 2
    step = SUB * width
    row_at = lax.broadcasted_iota(jnp.int32, (SUB * SUB, SUB * SUB), 0)
    col_at = lax.broadcasted_iota(jnp.int32, (SUB * SUB, SUB * SUB), 1)
    bits = SUB.bit_length() - 1
    swap = (col_at == ((row_at & (SUB - 1)) << bits) + (row_at >> bits)).astype(jnp.bfloat16)
    low = lax.broadcasted_iota(jnp.int32, (SUB, LANES), 1) < width
    groups = len(group_starts)
    lhs = jnp.concatenate(
        [
            turned_ref[pl.ds(pl.multiple_of(first + at, SUB), SUB), :]
            for first in (0, half)
            for at in group_starts
        ],
        axis=0,
    )
    chunks = extent // step
    sides = []
    for at in range(chunks):
        rhs = tiles_ref[:, :, at * step:(at + 1) * step].reshape(slots * width, step)
        acc = jnp.dot(lhs, rhs, preferred_element_type=jnp.float32)
        for s in range(groups):
            per_mu = []
            for q in range(step // LANES):
                a = acc[s * SUB:(s + 1) * SUB, q * LANES:(q + 1) * LANES]
                b = acc[(groups + s) * SUB:(groups + s + 1) * SUB, q * LANES:(q + 1) * LANES]
                per_mu.append(jnp.where(low, a, pltpu.roll(b, width, 1)).astype(jnp.bfloat16))
                per_mu.append(jnp.where(low, pltpu.roll(a, width, 1), b).astype(jnp.bfloat16))
            sides.append((at, s, jnp.concatenate(per_mu, axis=0)))
    moved = jnp.dot(
        swap, jnp.concatenate([side for _, _, side in sides], axis=1), preferred_element_type=jnp.float32
    ).astype(jnp.bfloat16)
    for n, (at, s, _) in enumerate(sides):
        for k in range(SUB):
            which, part, col = place(s, k)
            outs[which][part, at * SUB:(at + 1) * SUB, col * LANES:(col + 1) * LANES] = moved[
                k * SUB:(k + 1) * SUB, n * LANES:(n + 1) * LANES
            ]


def first_kernel(group_starts, place, n_parts, block_ref, tiles_ref, *refs):
    parts, (full_ref, turned_ref, *outs), picked = refs[:n_parts], refs[n_parts:-1], refs[-1]
    slots, width, _ = tiles_ref.shape
    depth = parts[0].shape[0]
    me = lax.axis_index("rep") if n_parts > 1 else 0
    for k in range(n_parts):
        full_ref[pl.ds(pl.multiple_of((me ^ k) * depth, depth), depth), :] = parts[k][...]
    for t in range(slots):
        row = pl.multiple_of(jnp.maximum(block_ref[0, t], 0) * width, width)
        rows = full_ref[pl.ds(row, width), :]
        picked[t * width:(t + 1) * width, :] = jnp.where(block_ref[0, t] >= 0, rows, jnp.zeros_like(rows))
    turned_ref[...] = picked[...].T
    multiply(turned_ref, tiles_ref, group_starts(), place, outs)


def next_kernel(group_starts, place, turned_ref, tiles_ref, skipped, *outs):
    multiply(turned_ref, tiles_ref, group_starts(), place, outs)


def contract_cost(tiles, norb, out_shapes):
    slots, width, extent = tiles.shape
    made = sum(math.prod(shape) for shape in out_shapes)
    return pl.CostEstimate(
        flops=2 * slots * width * made, bytes_accessed=2 * slots * width * extent + 2 * made, transcendentals=0
    )


def contract_first(group_starts, place, out_shapes, block, tiles, parts):
    slots, width, _ = tiles.shape
    depth, norb = parts[0].shape
    shapes = [(depth * len(parts), norb), (norb, slots * width)] + out_shapes
    full, turned, *made = pl.pallas_call(
        functools.partial(first_kernel, group_starts, place, len(parts)),
        out_shape=[jax.ShapeDtypeStruct(shape, jnp.bfloat16) for shape in shapes],
        in_specs=[pl.BlockSpec(memory_space=pltpu.VMEM)] * (2 + len(parts)),
        out_specs=[pl.BlockSpec(memory_space=pltpu.VMEM)] * len(shapes),
        scratch_shapes=[pltpu.VMEM((slots * width, norb), jnp.bfloat16)],
        compiler_params=pltpu.CompilerParams(vmem_limit_bytes=VMEM_LIMIT),
        cost_estimate=contract_cost(tiles, norb, out_shapes),
    )(block, tiles, *parts)
    return full, turned, made


def contract_next(group_starts, place, out_shapes, turned, tiles, after):
    return pl.pallas_call(
        functools.partial(next_kernel, group_starts, place),
        out_shape=[jax.ShapeDtypeStruct(shape, jnp.bfloat16) for shape in out_shapes],
        in_specs=[pl.BlockSpec(memory_space=pltpu.VMEM)] * 2 + [pl.BlockSpec(memory_space=pl.ANY)],
        out_specs=[pl.BlockSpec(memory_space=pltpu.VMEM)] * len(out_shapes),
        compiler_params=pltpu.CompilerParams(vmem_limit_bytes=VMEM_LIMIT),
        cost_estimate=contract_cost(tiles, turned.shape[0], out_shapes),
    )(turned, tiles, after)


def orbital_rows(orb_ref, width, ids):
    rows = [orb_ref[pl.ds(pl.multiple_of(b * width, width), width), :] for b in ids]
    return jnp.concatenate(rows, axis=0).T


def joined(refs, lanes=slice(None)):
    return jnp.concatenate([ref[:, :, lanes].reshape(-1, ref[:, :, lanes].shape[2]) for ref in refs], axis=0)


def fit_kernel(step, width, early_ids, late_ids, orb_ref, *refs):
    rows, (out_ref, *late_ref) = refs[:-1 - bool(late_ids)], refs[-1 - bool(late_ids):]
    turned = orbital_rows(orb_ref, width, early_ids())
    for at in range(out_ref.shape[1] // step):
        lanes = slice(at * step, (at + 1) * step)
        out_ref[:, lanes] = jnp.dot(turned, joined(rows, lanes), preferred_element_type=jnp.float32)
    if late_ids:
        late_ref[0][...] = orbital_rows(orb_ref, width, late_ids())


def fit(orbitals, early, n_late, early_ids, late_ids):
    width, cols = early[0].shape[1:]
    number = sum(each.shape[0] for each in early)
    norb = orbitals.shape[1]
    shapes = [jax.ShapeDtypeStruct((norb, cols), jnp.float32)]
    if n_late:
        shapes.append(jax.ShapeDtypeStruct((norb, n_late * width), jnp.bfloat16))
    return pl.pallas_call(
        functools.partial(fit_kernel, min(512, cols), width, early_ids, late_ids),
        out_shape=shapes,
        in_specs=[pl.BlockSpec(memory_space=pltpu.VMEM)] * (1 + len(early)),
        out_specs=[pl.BlockSpec(memory_space=pltpu.VMEM)] * len(shapes),
        compiler_params=pltpu.CompilerParams(vmem_limit_bytes=VMEM_LIMIT),
        cost_estimate=pl.CostEstimate(
            flops=2 * number * width * cols * norb,
            bytes_accessed=2 * number * width * cols + 4 * norb * cols,
            transcendentals=0,
        ),
    )(orbitals, *early)


def action_kernel(fit_scale, mix_scale, step, width, ids, n_early, n_late, fitted_ref, *refs):
    early, late, (keep_ref, send_ref, fitted) = refs[:n_early], refs[n_early:n_early + n_late], refs[-3:]
    norb, cols = fitted_ref.shape
    upper = lax.axis_index("rep") % 2 == 1
    if late:
        turned = refs[n_early + n_late][...]
    for at in range(cols // step):
        lanes = slice(at * step, (at + 1) * step)
        total = fitted_ref[:, lanes]
        if late:
            total = total + jnp.dot(turned, joined(late, lanes), preferred_element_type=jnp.float32)
        fitted[:, lanes] = (fit_scale * total).astype(jnp.bfloat16)
    term = lax.dot_general(
        joined(early + late), fitted[...], (((1,), (1,)), ((), ())), preferred_element_type=jnp.float32
    )
    blocks = ids()
    term = (-mix_scale * term).reshape(len(blocks), 2, width // 2, norb)
    keep = jnp.where(upper, term[:, 1], term[:, 0])
    send = jnp.where(upper, term[:, 0], term[:, 1])
    for k, b in enumerate(blocks):
        keep_ref[b] = keep[k]
        send_ref[b] = send[k]


def action(fitted, early, late, ids, basis_rows, fit_scale, mix_scale):
    norb, cols = fitted[0].shape
    width = early[0].shape[1]
    blocks = basis_rows // width
    shape = jax.ShapeDtypeStruct((blocks, width // 2, norb), jnp.float32)
    return pl.pallas_call(
        functools.partial(
            action_kernel, fit_scale, mix_scale, min(512, cols), width, ids, len(early), len(late)
        ),
        out_shape=[shape, shape],
        in_specs=[pl.BlockSpec(memory_space=pltpu.VMEM)] * (len(fitted) + len(early) + len(late)),
        out_specs=[pl.BlockSpec(memory_space=pltpu.VMEM)] * 2,
        scratch_shapes=[pltpu.VMEM((norb, cols), jnp.bfloat16)],
        compiler_params=pltpu.CompilerParams(vmem_limit_bytes=VMEM_LIMIT),
        cost_estimate=pl.CostEstimate(
            flops=4 * blocks * width * cols * norb, bytes_accessed=2 * blocks * width * cols, transcendentals=0
        ),
    )(fitted[0], *early, *late, *fitted[1:])


def swapped(x, axis, k):
    return lax.ppermute(x, axis, [(i, i ^ k) for i in range(lax.axis_size(axis))])


def per_device(orbitals, tiles, tile_block, tile_count):
    rep_size = lax.axis_size("rep")
    grid_size = lax.axis_size("grid")
    width = tiles.shape[3]
    depth, norb = orbitals.shape
    half = norb // 2
    cols = width * norb // grid_size
    basis_rows = depth * rep_size
    fit_scale = 1.0 / math.sqrt(basis_rows)
    mix_scale = 0.25 / math.sqrt(width * rep_size * norb)
    inside, block = load(tiles, tile_count, tile_block)
    per_part = half // grid_size
    if per_part == SUB and grid_size == 8 and rep_size == 4:
        near_size = grid_size // 2
        parts = [orbitals] + [swapped(orbitals, "rep", k) for k in range(1, rep_size)]

        def ids(ks):
            def blocks():
                me = lax.axis_index("grid")
                return [me ^ k for k in ks]

            return blocks

        def starts(ks):
            return lambda: [b * SUB for b in ids(ks)()]

        def own_output(s, k):
            return s, 0, k

        def shapes(ks):
            return [(1, width, cols)] * len(ks)

        waves, late_ks = [[6], [0, 1, 2, 3], [4, 5, 7]], [4, 5, 7]
        full, turned, made = contract_first(
            starts(waves[0]), own_output, shapes(waves[0]), block, inside, parts
        )
        sent = dict(zip(waves[0], made))
        for wave in waves[1:]:
            made = contract_next(starts(wave), own_output, shapes(wave), turned, inside, made[0])
            sent.update(zip(wave, made))
        received = {k: swapped(sent[k], "grid", k) if k else sent[k] for wave in waves for k in wave}
        early_ks = [k for wave in waves for k in wave if k not in late_ks]
        early, late = [received[k] for k in early_ks], [received[k] for k in late_ks]
        early_ids, late_ids, all_ids = ids(early_ks), ids(late_ks), ids(early_ks + late_ks)
    else:
        def place(s, k):
            part, col = divmod(s * SUB + k, per_part)
            return 0, part, col

        parts = [lax.all_gather(orbitals, "rep", axis=0, tiled=True)]
        full, _, (sent,) = contract_first(
            lambda: list(range(0, half, SUB)), place, [(grid_size, width, cols)], block, inside, parts
        )
        early, late = [lax.all_to_all(sent, "grid", 0, 0, tiled=True)], []

        def early_ids():
            return list(range(grid_size))

        late_ids, all_ids = None, early_ids
    fitted = fit(full, early, len(late), early_ids, late_ids)
    part_keep, part_send = action(fitted, early, late, all_ids, basis_rows, fit_scale, mix_scale)
    pair = part_keep + swapped(part_send, "rep", 1)
    mine = jnp.sum(lax.all_to_all(pair, "grid", 0, 0, tiled=True), axis=0)
    if rep_size == 4:
        other, across = swapped(mine, "rep", 2), swapped(mine, "rep", 3)
        beside = swapped(mine, "rep", 1)
        own, theirs = mine + other, beside + across
        upper = lax.axis_index("rep") % 2 == 1
        return jnp.concatenate([jnp.where(upper, theirs, own), jnp.where(upper, own, theirs)], axis=0)
    every = lax.all_gather(mine, "rep", axis=0, tiled=False)
    return jnp.sum(every.reshape(rep_size // 2, 2, width // 2, norb), axis=0).reshape(width, norb)


def solution(mesh):
    in_specs = (
        P("rep", None),
        P("rep", "grid", None, None, None),
        P("rep", "grid", None),
        P("rep", "grid"),
    )
    return jax.shard_map(
        per_device, mesh=mesh, in_specs=in_specs, out_specs=P("grid", None), check_vma=False
    )
```

```python
import functools
import math

import jax
import jax.numpy as jnp
from jax import lax
from jax.experimental import pallas as pl
from jax.experimental.pallas import tpu as pltpu
from jax.sharding import PartitionSpec as P

LANES = 128
SUB = 16
VMEM_LIMIT = 24 * 1024 * 1024


def load_kernel(count_ref, block_hbm, tiles_hbm, out_ref, live_ref, block, sems, block_sem):
    chunks = sems.shape[0]
    step = out_ref.shape[2] // chunks
    copies = [
        pltpu.make_async_copy(
            tiles_hbm.at[0, 0, :, :, pl.ds(at * step, step)], out_ref.at[:, :, pl.ds(at * step, step)], sems.at[at]
        )
        for at in range(chunks)
    ]
    block_copy = pltpu.make_async_copy(block_hbm, block, block_sem.at[0])
    block_copy.start()
    for each in copies:
        each.start()
    block_copy.wait()
    slot = lax.broadcasted_iota(jnp.int32, live_ref.shape, 1)
    live_ref[...] = jnp.where(slot < count_ref[0, 0], block[0], -1)
    for each in copies:
        each.wait()


def in_hbm(x):
    return pltpu.with_memory_space_constraint(x, pltpu.HBM)


def load(tiles, count, block):
    return pl.pallas_call(
        load_kernel,
        out_shape=[
            jax.ShapeDtypeStruct(tiles.shape[2:], tiles.dtype),
            jax.ShapeDtypeStruct(block.shape[1:], block.dtype),
        ],
        in_specs=[
            pl.BlockSpec(memory_space=pltpu.SMEM),
            pl.BlockSpec(memory_space=pltpu.HBM),
            pl.BlockSpec(memory_space=pltpu.HBM),
        ],
        out_specs=[pl.BlockSpec(memory_space=pltpu.VMEM)] * 2,
        scratch_shapes=[
            pltpu.VMEM(block.shape, block.dtype),
            pltpu.SemaphoreType.DMA((4,)),
            pltpu.SemaphoreType.DMA((1,)),
        ],
        compiler_params=pltpu.CompilerParams(vmem_limit_bytes=VMEM_LIMIT),
        cost_estimate=pl.CostEstimate(flops=0, bytes_accessed=2 * math.prod(tiles.shape), transcendentals=0),
    )(count, in_hbm(block), in_hbm(tiles))


def multiply(turned_ref, tiles_ref, group_starts, place, outs):
    slots, width, extent = tiles_ref.shape
    half = turned_ref.shape[0] // 2
    step = SUB * width
    row_at = lax.broadcasted_iota(jnp.int32, (SUB * SUB, SUB * SUB), 0)
    col_at = lax.broadcasted_iota(jnp.int32, (SUB * SUB, SUB * SUB), 1)
    bits = SUB.bit_length() - 1
    swap = (col_at == ((row_at & (SUB - 1)) << bits) + (row_at >> bits)).astype(jnp.bfloat16)
    low = lax.broadcasted_iota(jnp.int32, (SUB, LANES), 1) < width
    groups = len(group_starts)
    lhs = jnp.concatenate(
        [
            turned_ref[pl.ds(pl.multiple_of(first + at, SUB), SUB), :]
            for first in (0, half)
            for at in group_starts
        ],
        axis=0,
    )
    chunks = extent // step
    sides = []
    for at in range(chunks):
        rhs = tiles_ref[:, :, at * step:(at + 1) * step].reshape(slots * width, step)
        acc = jnp.dot(lhs, rhs, preferred_element_type=jnp.float32)
        for s in range(groups):
            per_mu = []
            for q in range(step // LANES):
                a = acc[s * SUB:(s + 1) * SUB, q * LANES:(q + 1) * LANES]
                b = acc[(groups + s) * SUB:(groups + s + 1) * SUB, q * LANES:(q + 1) * LANES]
                per_mu.append(jnp.where(low, a, pltpu.roll(b, width, 1)).astype(jnp.bfloat16))
                per_mu.append(jnp.where(low, pltpu.roll(a, width, 1), b).astype(jnp.bfloat16))
            sides.append((at, s, jnp.concatenate(per_mu, axis=0)))
    moved = jnp.dot(
        swap, jnp.concatenate([side for _, _, side in sides], axis=1), preferred_element_type=jnp.float32
    ).astype(jnp.bfloat16)
    for n, (at, s, _) in enumerate(sides):
        for k in range(SUB):
            which, part, col = place(s, k)
            outs[which][part, at * SUB:(at + 1) * SUB, col * LANES:(col + 1) * LANES] = moved[
                k * SUB:(k + 1) * SUB, n * LANES:(n + 1) * LANES
            ]


def first_kernel(group_starts, place, n_parts, block_ref, tiles_ref, *refs):
    parts, (full_ref, turned_ref, *outs), picked = refs[:n_parts], refs[n_parts:-1], refs[-1]
    slots, width, _ = tiles_ref.shape
    depth = parts[0].shape[0]
    me = lax.axis_index("rep") if n_parts > 1 else 0
    for k in range(n_parts):
        full_ref[pl.ds(pl.multiple_of((me ^ k) * depth, depth), depth), :] = parts[k][...]
    for t in range(slots):
        row = pl.multiple_of(jnp.maximum(block_ref[0, t], 0) * width, width)
        rows = full_ref[pl.ds(row, width), :]
        picked[t * width:(t + 1) * width, :] = jnp.where(block_ref[0, t] >= 0, rows, jnp.zeros_like(rows))
    turned_ref[...] = picked[...].T
    multiply(turned_ref, tiles_ref, group_starts(), place, outs)


def next_kernel(group_starts, place, turned_ref, tiles_ref, skipped, *outs):
    multiply(turned_ref, tiles_ref, group_starts(), place, outs)


def contract_cost(tiles, norb, out_shapes):
    slots, width, extent = tiles.shape
    made = sum(math.prod(shape) for shape in out_shapes)
    return pl.CostEstimate(
        flops=2 * slots * width * made, bytes_accessed=2 * slots * width * extent + 2 * made, transcendentals=0
    )


def contract_first(group_starts, place, out_shapes, block, tiles, parts):
    slots, width, _ = tiles.shape
    depth, norb = parts[0].shape
    shapes = [(depth * len(parts), norb), (norb, slots * width)] + out_shapes
    full, turned, *made = pl.pallas_call(
        functools.partial(first_kernel, group_starts, place, len(parts)),
        out_shape=[jax.ShapeDtypeStruct(shape, jnp.bfloat16) for shape in shapes],
        in_specs=[pl.BlockSpec(memory_space=pltpu.VMEM)] * (2 + len(parts)),
        out_specs=[pl.BlockSpec(memory_space=pltpu.VMEM)] * len(shapes),
        scratch_shapes=[pltpu.VMEM((slots * width, norb), jnp.bfloat16)],
        compiler_params=pltpu.CompilerParams(vmem_limit_bytes=VMEM_LIMIT),
        cost_estimate=contract_cost(tiles, norb, out_shapes),
    )(block, tiles, *parts)
    return full, turned, made


def contract_next(group_starts, place, out_shapes, turned, tiles, after):
    return pl.pallas_call(
        functools.partial(next_kernel, group_starts, place),
        out_shape=[jax.ShapeDtypeStruct(shape, jnp.bfloat16) for shape in out_shapes],
        in_specs=[pl.BlockSpec(memory_space=pltpu.VMEM)] * 2 + [pl.BlockSpec(memory_space=pl.ANY)],
        out_specs=[pl.BlockSpec(memory_space=pltpu.VMEM)] * len(out_shapes),
        compiler_params=pltpu.CompilerParams(vmem_limit_bytes=VMEM_LIMIT),
        cost_estimate=contract_cost(tiles, turned.shape[0], out_shapes),
    )(turned, tiles, after)


def orbital_rows(orb_ref, width, ids):
    rows = [orb_ref[pl.ds(pl.multiple_of(b * width, width), width), :] for b in ids]
    return jnp.concatenate(rows, axis=0).T


def joined(refs, lanes=slice(None)):
    return jnp.concatenate([ref[:, :, lanes].reshape(-1, ref[:, :, lanes].shape[2]) for ref in refs], axis=0)


def fit_kernel(step, width, early_ids, late_ids, orb_ref, *refs):
    rows, (out_ref, *late_ref) = refs[:-1 - bool(late_ids)], refs[-1 - bool(late_ids):]
    turned = orbital_rows(orb_ref, width, early_ids())
    for at in range(out_ref.shape[1] // step):
        lanes = slice(at * step, (at + 1) * step)
        out_ref[:, lanes] = jnp.dot(turned, joined(rows, lanes), preferred_element_type=jnp.float32)
    if late_ids:
        late_ref[0][...] = orbital_rows(orb_ref, width, late_ids())


def fit(orbitals, early, n_late, early_ids, late_ids):
    width, cols = early[0].shape[1:]
    number = sum(each.shape[0] for each in early)
    norb = orbitals.shape[1]
    shapes = [jax.ShapeDtypeStruct((norb, cols), jnp.float32)]
    if n_late:
        shapes.append(jax.ShapeDtypeStruct((norb, n_late * width), jnp.bfloat16))
    return pl.pallas_call(
        functools.partial(fit_kernel, min(512, cols), width, early_ids, late_ids),
        out_shape=shapes,
        in_specs=[pl.BlockSpec(memory_space=pltpu.VMEM)] * (1 + len(early)),
        out_specs=[pl.BlockSpec(memory_space=pltpu.VMEM)] * len(shapes),
        compiler_params=pltpu.CompilerParams(vmem_limit_bytes=VMEM_LIMIT),
        cost_estimate=pl.CostEstimate(
            flops=2 * number * width * cols * norb,
            bytes_accessed=2 * number * width * cols + 4 * norb * cols,
            transcendentals=0,
        ),
    )(orbitals, *early)


def action_kernel(fit_scale, mix_scale, step, width, ids, n_early, n_late, fitted_ref, *refs):
    early, late, (keep_ref, send_ref, fitted) = refs[:n_early], refs[n_early:n_early + n_late], refs[-3:]
    norb, cols = fitted_ref.shape
    upper = lax.axis_index("rep") % 2 == 1
    if late:
        turned = refs[n_early + n_late][...]
    for at in range(cols // step):
        lanes = slice(at * step, (at + 1) * step)
        total = fitted_ref[:, lanes]
        if late:
            total = total + jnp.dot(turned, joined(late, lanes), preferred_element_type=jnp.float32)
        fitted[:, lanes] = (fit_scale * total).astype(jnp.bfloat16)
    term = lax.dot_general(
        joined(early + late), fitted[...], (((1,), (1,)), ((), ())), preferred_element_type=jnp.float32
    )
    blocks = ids()
    term = (-mix_scale * term).reshape(len(blocks), 2, width // 2, norb)
    keep = jnp.where(upper, term[:, 1], term[:, 0])
    send = jnp.where(upper, term[:, 0], term[:, 1])
    for k, b in enumerate(blocks):
        keep_ref[b] = keep[k]
        send_ref[b] = send[k]


def action(fitted, early, late, ids, basis_rows, fit_scale, mix_scale):
    norb, cols = fitted[0].shape
    width = early[0].shape[1]
    blocks = basis_rows // width
    shape = jax.ShapeDtypeStruct((blocks, width // 2, norb), jnp.float32)
    return pl.pallas_call(
        functools.partial(
            action_kernel, fit_scale, mix_scale, min(512, cols), width, ids, len(early), len(late)
        ),
        out_shape=[shape, shape],
        in_specs=[pl.BlockSpec(memory_space=pltpu.VMEM)] * (len(fitted) + len(early) + len(late)),
        out_specs=[pl.BlockSpec(memory_space=pltpu.VMEM)] * 2,
        scratch_shapes=[pltpu.VMEM((norb, cols), jnp.bfloat16)],
        compiler_params=pltpu.CompilerParams(vmem_limit_bytes=VMEM_LIMIT),
        cost_estimate=pl.CostEstimate(
            flops=4 * blocks * width * cols * norb, bytes_accessed=2 * blocks * width * cols, transcendentals=0
        ),
    )(fitted[0], *early, *late, *fitted[1:])


def swapped(x, axis, k):
    return lax.ppermute(x, axis, [(i, i ^ k) for i in range(lax.axis_size(axis))])


def summed_blocks(blocks, axis):
    rows = blocks.shape[1]
    largest = jnp.max(jnp.abs(blocks), axis=1, keepdims=True)
    exponent = jnp.ceil(jnp.log2(jnp.maximum(largest, 1e-30)))
    scaled = (blocks * jnp.exp2(-exponent)).astype(jnp.float16)
    tail = jnp.broadcast_to(exponent.astype(jnp.float16), (blocks.shape[0], 8, blocks.shape[2]))
    got = lax.all_to_all(jnp.concatenate([scaled, tail], axis=1), axis, 0, 0, tiled=True).astype(jnp.float32)
    return jnp.sum(got[:, :rows] * jnp.exp2(got[:, rows:rows + 1]), axis=0)


def per_device(orbitals, tiles, tile_block, tile_count):
    rep_size = lax.axis_size("rep")
    grid_size = lax.axis_size("grid")
    width = tiles.shape[3]
    depth, norb = orbitals.shape
    half = norb // 2
    cols = width * norb // grid_size
    basis_rows = depth * rep_size
    fit_scale = 1.0 / math.sqrt(basis_rows)
    mix_scale = 0.25 / math.sqrt(width * rep_size * norb)
    inside, block = load(tiles, tile_count, tile_block)
    per_part = half // grid_size
    if per_part == SUB and grid_size == 8 and rep_size == 4:
        near_size = grid_size // 2
        parts = [orbitals] + [swapped(orbitals, "rep", k) for k in range(1, rep_size)]

        def ids(ks):
            def blocks():
                me = lax.axis_index("grid")
                return [me ^ k for k in ks]

            return blocks

        def starts(ks):
            return lambda: [b * SUB for b in ids(ks)()]

        def own_output(s, k):
            return s, 0, k

        def shapes(ks):
            return [(1, width, cols)] * len(ks)

        waves, late_ks = [[6], [0, 1, 2, 3], [5, 4, 7]], [5, 4, 7]
        full, turned, made = contract_first(
            starts(waves[0]), own_output, shapes(waves[0]), block, inside, parts
        )
        sent = dict(zip(waves[0], made))
        for wave in waves[1:]:
            made = contract_next(starts(wave), own_output, shapes(wave), turned, inside, made[0])
            sent.update(zip(wave, made))
        received = {k: swapped(sent[k], "grid", k) if k else sent[k] for wave in waves for k in wave}
        early_ks = [k for wave in waves for k in wave if k not in late_ks]
        early, late = [received[k] for k in early_ks], [received[k] for k in late_ks]
        early_ids, late_ids, all_ids = ids(early_ks), ids(late_ks), ids(early_ks + late_ks)
    else:
        def place(s, k):
            part, col = divmod(s * SUB + k, per_part)
            return 0, part, col

        parts = [lax.all_gather(orbitals, "rep", axis=0, tiled=True)]
        full, _, (sent,) = contract_first(
            lambda: list(range(0, half, SUB)), place, [(grid_size, width, cols)], block, inside, parts
        )
        early, late = [lax.all_to_all(sent, "grid", 0, 0, tiled=True)], []

        def early_ids():
            return list(range(grid_size))

        late_ids, all_ids = None, early_ids
    fitted = fit(full, early, len(late), early_ids, late_ids)
    part_keep, part_send = action(fitted, early, late, all_ids, basis_rows, fit_scale, mix_scale)
    pair = part_keep + swapped(part_send, "rep", 1)
    mine = summed_blocks(pair, "grid")
    if rep_size == 4:
        other, across = swapped(mine, "rep", 2), swapped(mine, "rep", 3)
        beside = swapped(mine, "rep", 1)
        own, theirs = mine + other, beside + across
        upper = lax.axis_index("rep") % 2 == 1
        return jnp.concatenate([jnp.where(upper, theirs, own), jnp.where(upper, own, theirs)], axis=0)
    every = lax.all_gather(mine, "rep", axis=0, tiled=False)
    return jnp.sum(every.reshape(rep_size // 2, 2, width // 2, norb), axis=0).reshape(width, norb)


def solution(mesh):
    in_specs = (
        P("rep", None),
        P("rep", "grid", None, None, None),
        P("rep", "grid", None),
        P("rep", "grid"),
    )
    return jax.shard_map(
        per_device, mesh=mesh, in_specs=in_specs, out_specs=P("grid", None), check_vma=False
    )
```

```python
import functools
import math

import jax
import jax.numpy as jnp
from jax import lax
from jax.experimental import pallas as pl
from jax.experimental.pallas import tpu as pltpu
from jax.sharding import PartitionSpec as P

LANES = 128
SUB = 16
VMEM_LIMIT = 24 * 1024 * 1024


def load_kernel(count_ref, block_hbm, tiles_hbm, out_ref, live_ref, block, sems, block_sem):
    chunks = sems.shape[0]
    step = out_ref.shape[2] // chunks
    copies = [
        pltpu.make_async_copy(
            tiles_hbm.at[0, 0, :, :, pl.ds(at * step, step)], out_ref.at[:, :, pl.ds(at * step, step)], sems.at[at]
        )
        for at in range(chunks)
    ]
    block_copy = pltpu.make_async_copy(block_hbm, block, block_sem.at[0])
    block_copy.start()
    for each in copies:
        each.start()
    block_copy.wait()
    slot = lax.broadcasted_iota(jnp.int32, live_ref.shape, 1)
    live_ref[...] = jnp.where(slot < count_ref[0, 0], block[0], -1)
    for each in copies:
        each.wait()


def in_hbm(x):
    return pltpu.with_memory_space_constraint(x, pltpu.HBM)


def load(tiles, count, block):
    return pl.pallas_call(
        load_kernel,
        out_shape=[
            jax.ShapeDtypeStruct(tiles.shape[2:], tiles.dtype),
            jax.ShapeDtypeStruct(block.shape[1:], block.dtype),
        ],
        in_specs=[
            pl.BlockSpec(memory_space=pltpu.SMEM),
            pl.BlockSpec(memory_space=pltpu.HBM),
            pl.BlockSpec(memory_space=pltpu.HBM),
        ],
        out_specs=[pl.BlockSpec(memory_space=pltpu.VMEM)] * 2,
        scratch_shapes=[
            pltpu.VMEM(block.shape, block.dtype),
            pltpu.SemaphoreType.DMA((4,)),
            pltpu.SemaphoreType.DMA((1,)),
        ],
        compiler_params=pltpu.CompilerParams(vmem_limit_bytes=VMEM_LIMIT),
        cost_estimate=pl.CostEstimate(flops=0, bytes_accessed=2 * math.prod(tiles.shape), transcendentals=0),
    )(count, in_hbm(block), in_hbm(tiles))


def multiply(turned_ref, tiles_ref, group_starts, place, outs):
    slots, width, extent = tiles_ref.shape
    half = turned_ref.shape[0] // 2
    step = SUB * width
    row_at = lax.broadcasted_iota(jnp.int32, (SUB * SUB, SUB * SUB), 0)
    col_at = lax.broadcasted_iota(jnp.int32, (SUB * SUB, SUB * SUB), 1)
    bits = SUB.bit_length() - 1
    swap = (col_at == ((row_at & (SUB - 1)) << bits) + (row_at >> bits)).astype(jnp.bfloat16)
    low = lax.broadcasted_iota(jnp.int32, (SUB, LANES), 1) < width
    groups = len(group_starts)
    lhs = jnp.concatenate(
        [
            turned_ref[pl.ds(pl.multiple_of(first + at, SUB), SUB), :]
            for first in (0, half)
            for at in group_starts
        ],
        axis=0,
    )
    chunks = extent // step
    sides = []
    for at in range(chunks):
        rhs = tiles_ref[:, :, at * step:(at + 1) * step].reshape(slots * width, step)
        acc = jnp.dot(lhs, rhs, preferred_element_type=jnp.float32)
        for s in range(groups):
            per_mu = []
            for q in range(step // LANES):
                a = acc[s * SUB:(s + 1) * SUB, q * LANES:(q + 1) * LANES]
                b = acc[(groups + s) * SUB:(groups + s + 1) * SUB, q * LANES:(q + 1) * LANES]
                per_mu.append(jnp.where(low, a, pltpu.roll(b, width, 1)).astype(jnp.bfloat16))
                per_mu.append(jnp.where(low, pltpu.roll(a, width, 1), b).astype(jnp.bfloat16))
            sides.append((at, s, jnp.concatenate(per_mu, axis=0)))
    moved = jnp.dot(
        swap, jnp.concatenate([side for _, _, side in sides], axis=1), preferred_element_type=jnp.float32
    ).astype(jnp.bfloat16)
    for n, (at, s, _) in enumerate(sides):
        for k in range(SUB):
            which, part, col = place(s, k)
            outs[which][part, at * SUB:(at + 1) * SUB, col * LANES:(col + 1) * LANES] = moved[
                k * SUB:(k + 1) * SUB, n * LANES:(n + 1) * LANES
            ]


def first_kernel(group_starts, place, n_parts, block_ref, tiles_ref, *refs):
    parts, (full_ref, turned_ref, *outs), picked = refs[:n_parts], refs[n_parts:-1], refs[-1]
    slots, width, _ = tiles_ref.shape
    depth = parts[0].shape[0]
    me = lax.axis_index("rep") if n_parts > 1 else 0
    for k in range(n_parts):
        full_ref[pl.ds(pl.multiple_of((me ^ k) * depth, depth), depth), :] = parts[k][...]
    for t in range(slots):
        row = pl.multiple_of(jnp.maximum(block_ref[0, t], 0) * width, width)
        rows = full_ref[pl.ds(row, width), :]
        picked[t * width:(t + 1) * width, :] = jnp.where(block_ref[0, t] >= 0, rows, jnp.zeros_like(rows))
    turned_ref[...] = picked[...].T
    multiply(turned_ref, tiles_ref, group_starts(), place, outs)


def next_kernel(group_starts, place, turned_ref, tiles_ref, skipped, *outs):
    multiply(turned_ref, tiles_ref, group_starts(), place, outs)


def contract_cost(tiles, norb, out_shapes):
    slots, width, extent = tiles.shape
    made = sum(math.prod(shape) for shape in out_shapes)
    return pl.CostEstimate(
        flops=2 * slots * width * made, bytes_accessed=2 * slots * width * extent + 2 * made, transcendentals=0
    )


def contract_first(group_starts, place, out_shapes, block, tiles, parts):
    slots, width, _ = tiles.shape
    depth, norb = parts[0].shape
    shapes = [(depth * len(parts), norb), (norb, slots * width)] + out_shapes
    full, turned, *made = pl.pallas_call(
        functools.partial(first_kernel, group_starts, place, len(parts)),
        out_shape=[jax.ShapeDtypeStruct(shape, jnp.bfloat16) for shape in shapes],
        in_specs=[pl.BlockSpec(memory_space=pltpu.VMEM)] * (2 + len(parts)),
        out_specs=[pl.BlockSpec(memory_space=pltpu.VMEM)] * len(shapes),
        scratch_shapes=[pltpu.VMEM((slots * width, norb), jnp.bfloat16)],
        compiler_params=pltpu.CompilerParams(vmem_limit_bytes=VMEM_LIMIT),
        cost_estimate=contract_cost(tiles, norb, out_shapes),
    )(block, tiles, *parts)
    return full, turned, made


def contract_next(group_starts, place, out_shapes, turned, tiles, after):
    return pl.pallas_call(
        functools.partial(next_kernel, group_starts, place),
        out_shape=[jax.ShapeDtypeStruct(shape, jnp.bfloat16) for shape in out_shapes],
        in_specs=[pl.BlockSpec(memory_space=pltpu.VMEM)] * 2 + [pl.BlockSpec(memory_space=pl.ANY)],
        out_specs=[pl.BlockSpec(memory_space=pltpu.VMEM)] * len(out_shapes),
        compiler_params=pltpu.CompilerParams(vmem_limit_bytes=VMEM_LIMIT),
        cost_estimate=contract_cost(tiles, turned.shape[0], out_shapes),
    )(turned, tiles, after)


def orbital_rows(orb_ref, width, ids):
    rows = [orb_ref[pl.ds(pl.multiple_of(b * width, width), width), :] for b in ids]
    return jnp.concatenate(rows, axis=0).T


def joined(refs, lanes=slice(None)):
    return jnp.concatenate([ref[:, :, lanes].reshape(-1, ref[:, :, lanes].shape[2]) for ref in refs], axis=0)


def fit_kernel(step, width, early_ids, late_ids, orb_ref, *refs):
    rows, (out_ref, *late_ref) = refs[:-1 - bool(late_ids)], refs[-1 - bool(late_ids):]
    turned = orbital_rows(orb_ref, width, early_ids())
    for at in range(out_ref.shape[1] // step):
        lanes = slice(at * step, (at + 1) * step)
        out_ref[:, lanes] = jnp.dot(turned, joined(rows, lanes), preferred_element_type=jnp.float32)
    if late_ids:
        late_ref[0][...] = orbital_rows(orb_ref, width, late_ids())


def fit(orbitals, early, n_late, early_ids, late_ids):
    width, cols = early[0].shape[1:]
    number = sum(each.shape[0] for each in early)
    norb = orbitals.shape[1]
    shapes = [jax.ShapeDtypeStruct((norb, cols), jnp.float32)]
    if n_late:
        shapes.append(jax.ShapeDtypeStruct((norb, n_late * width), jnp.bfloat16))
    return pl.pallas_call(
        functools.partial(fit_kernel, min(512, cols), width, early_ids, late_ids),
        out_shape=shapes,
        in_specs=[pl.BlockSpec(memory_space=pltpu.VMEM)] * (1 + len(early)),
        out_specs=[pl.BlockSpec(memory_space=pltpu.VMEM)] * len(shapes),
        compiler_params=pltpu.CompilerParams(vmem_limit_bytes=VMEM_LIMIT),
        cost_estimate=pl.CostEstimate(
            flops=2 * number * width * cols * norb,
            bytes_accessed=2 * number * width * cols + 4 * norb * cols,
            transcendentals=0,
        ),
    )(orbitals, *early)


def action_half(rows, fitted, mix_scale, half, width, ids, out_ref):
    offset = pl.multiple_of(half * (width // 2), width // 2)
    lhs = jnp.concatenate(
        [ref[b, pl.ds(offset, width // 2), :] for ref in rows for b in range(ref.shape[0])], axis=0
    )
    term = lax.dot_general(lhs, fitted, (((1,), (1,)), ((), ())), preferred_element_type=jnp.float32)
    term = (-mix_scale * term).reshape((-1,) + out_ref.shape[1:])
    for k, b in enumerate(ids):
        out_ref[b] = term[k]


def send_kernel(fit_scale, mix_scale, step, width, ids, n_early, n_late, fitted_ref, *refs):
    rows, late, (send_ref, out_ref) = refs[:n_early + n_late], refs[n_early:n_early + n_late], refs[-2:]
    cols = fitted_ref.shape[1]
    if late:
        turned = refs[n_early + n_late][...]
    for at in range(cols // step):
        lanes = slice(at * step, (at + 1) * step)
        total = fitted_ref[:, lanes]
        if late:
            total = total + jnp.dot(turned, joined(late, lanes), preferred_element_type=jnp.float32)
        out_ref[:, lanes] = (fit_scale * total).astype(jnp.bfloat16)
    core = lax.axis_index("rep") % 2
    action_half(rows, out_ref[...], mix_scale, 1 - core, width, ids(), send_ref)


def keep_kernel(mix_scale, width, ids, fitted_ref, *refs):
    core = lax.axis_index("rep") % 2
    action_half(refs[:-1], fitted_ref[...], mix_scale, core, width, ids(), refs[-1])


def action(fitted, early, late, ids, basis_rows, fit_scale, mix_scale):
    norb, cols = fitted[0].shape
    width = early[0].shape[1]
    blocks = basis_rows // width
    half = jax.ShapeDtypeStruct((blocks, width // 2, norb), jnp.float32)
    rows = list(early) + list(late)
    params = pltpu.CompilerParams(vmem_limit_bytes=VMEM_LIMIT)
    cost = pl.CostEstimate(
        flops=2 * blocks * width * cols * norb, bytes_accessed=2 * blocks * width * cols, transcendentals=0
    )
    send, columns = pl.pallas_call(
        functools.partial(
            send_kernel, fit_scale, mix_scale, min(512, cols), width, ids, len(early), len(late)
        ),
        out_shape=[half, jax.ShapeDtypeStruct((norb, cols), jnp.bfloat16)],
        in_specs=[pl.BlockSpec(memory_space=pltpu.VMEM)] * (len(fitted) + len(rows)),
        out_specs=[pl.BlockSpec(memory_space=pltpu.VMEM)] * 2,
        compiler_params=params,
        cost_estimate=cost,
    )(fitted[0], *rows, *fitted[1:])
    keep = pl.pallas_call(
        functools.partial(keep_kernel, mix_scale, width, ids),
        out_shape=half,
        in_specs=[pl.BlockSpec(memory_space=pltpu.VMEM)] * (1 + len(rows)),
        out_specs=pl.BlockSpec(memory_space=pltpu.VMEM),
        compiler_params=params,
        cost_estimate=cost,
    )(columns, *rows)
    return keep, send


def swapped(x, axis, k):
    return lax.ppermute(x, axis, [(i, i ^ k) for i in range(lax.axis_size(axis))])


def summed_blocks(blocks, axis):
    rows = blocks.shape[1]
    largest = jnp.max(jnp.abs(blocks), axis=1, keepdims=True)
    exponent = jnp.ceil(jnp.log2(jnp.maximum(largest, 1e-30))) - 14
    scaled = (blocks * jnp.exp2(-exponent)).astype(jnp.float16)
    tail = jnp.broadcast_to(exponent.astype(jnp.float16), (blocks.shape[0], 8, blocks.shape[2]))
    got = lax.all_to_all(jnp.concatenate([scaled, tail], axis=1), axis, 0, 0, tiled=True).astype(jnp.float32)
    return jnp.sum(got[:, :rows] * jnp.exp2(got[:, rows:rows + 1]), axis=0)


def per_device(orbitals, tiles, tile_block, tile_count):
    rep_size = lax.axis_size("rep")
    grid_size = lax.axis_size("grid")
    width = tiles.shape[3]
    depth, norb = orbitals.shape
    half = norb // 2
    cols = width * norb // grid_size
    basis_rows = depth * rep_size
    fit_scale = 1.0 / math.sqrt(basis_rows)
    mix_scale = 0.25 / math.sqrt(width * rep_size * norb)
    inside, block = load(tiles, tile_count, tile_block)
    per_part = half // grid_size
    if per_part == SUB and grid_size == 8 and rep_size == 4:
        near_size = grid_size // 2
        parts = [orbitals] + [swapped(orbitals, "rep", k) for k in range(1, rep_size)]

        def ids(ks):
            def blocks():
                me = lax.axis_index("grid")
                return [me ^ k for k in ks]

            return blocks

        def starts(ks):
            return lambda: [b * SUB for b in ids(ks)()]

        def own_output(s, k):
            return s, 0, k

        def shapes(ks):
            return [(1, width, cols)] * len(ks)

        waves, late_ks = [[6], [0, 1, 2, 3], [5, 4, 7]], [5, 4, 7]
        full, turned, made = contract_first(
            starts(waves[0]), own_output, shapes(waves[0]), block, inside, parts
        )
        sent = dict(zip(waves[0], made))
        for wave in waves[1:]:
            made = contract_next(starts(wave), own_output, shapes(wave), turned, inside, made[0])
            sent.update(zip(wave, made))
        received = {k: swapped(sent[k], "grid", k) if k else sent[k] for wave in waves for k in wave}
        early_ks = [k for wave in waves for k in wave if k not in late_ks]
        early, late = [received[k] for k in early_ks], [received[k] for k in late_ks]
        early_ids, late_ids, all_ids = ids(early_ks), ids(late_ks), ids(early_ks + late_ks)
    else:
        def place(s, k):
            part, col = divmod(s * SUB + k, per_part)
            return 0, part, col

        parts = [lax.all_gather(orbitals, "rep", axis=0, tiled=True)]
        full, _, (sent,) = contract_first(
            lambda: list(range(0, half, SUB)), place, [(grid_size, width, cols)], block, inside, parts
        )
        early, late = [lax.all_to_all(sent, "grid", 0, 0, tiled=True)], []

        def early_ids():
            return list(range(grid_size))

        late_ids, all_ids = None, early_ids
    fitted = fit(full, early, len(late), early_ids, late_ids)
    part_keep, part_send = action(fitted, early, late, all_ids, basis_rows, fit_scale, mix_scale)
    pair = part_keep + swapped(part_send, "rep", 1)
    mine = summed_blocks(pair, "grid")
    if rep_size == 4:
        other, across = swapped(mine, "rep", 2), swapped(mine, "rep", 3)
        beside = swapped(mine, "rep", 1)
        own, theirs = mine + other, beside + across
        upper = lax.axis_index("rep") % 2 == 1
        return jnp.concatenate([jnp.where(upper, theirs, own), jnp.where(upper, own, theirs)], axis=0)
    every = lax.all_gather(mine, "rep", axis=0, tiled=False)
    return jnp.sum(every.reshape(rep_size // 2, 2, width // 2, norb), axis=0).reshape(width, norb)


def solution(mesh):
    in_specs = (
        P("rep", None),
        P("rep", "grid", None, None, None),
        P("rep", "grid", None),
        P("rep", "grid"),
    )
    return jax.shard_map(
        per_device, mesh=mesh, in_specs=in_specs, out_specs=P("grid", None), check_vma=False
    )
```

```python
import functools
import math

import jax
import jax.numpy as jnp
from jax import lax
from jax.experimental import pallas as pl
from jax.experimental.pallas import tpu as pltpu
from jax.sharding import PartitionSpec as P

LANES = 128
SUB = 16
VMEM_LIMIT = 24 * 1024 * 1024


def load_kernel(count_ref, block_hbm, tiles_hbm, out_ref, live_ref, block, sems, block_sem):
    chunks = sems.shape[0]
    step = out_ref.shape[2] // chunks
    copies = [
        pltpu.make_async_copy(
            tiles_hbm.at[0, 0, :, :, pl.ds(at * step, step)], out_ref.at[:, :, pl.ds(at * step, step)], sems.at[at]
        )
        for at in range(chunks)
    ]
    block_copy = pltpu.make_async_copy(block_hbm, block, block_sem.at[0])
    block_copy.start()
    for each in copies:
        each.start()
    block_copy.wait()
    slot = lax.broadcasted_iota(jnp.int32, live_ref.shape, 1)
    live_ref[...] = jnp.where(slot < count_ref[0, 0], block[0], -1)
    for each in copies:
        each.wait()


def in_hbm(x):
    return pltpu.with_memory_space_constraint(x, pltpu.HBM)


def load(tiles, count, block):
    return pl.pallas_call(
        load_kernel,
        out_shape=[
            jax.ShapeDtypeStruct(tiles.shape[2:], tiles.dtype),
            jax.ShapeDtypeStruct(block.shape[1:], block.dtype),
        ],
        in_specs=[
            pl.BlockSpec(memory_space=pltpu.SMEM),
            pl.BlockSpec(memory_space=pltpu.HBM),
            pl.BlockSpec(memory_space=pltpu.HBM),
        ],
        out_specs=[pl.BlockSpec(memory_space=pltpu.VMEM)] * 2,
        scratch_shapes=[
            pltpu.VMEM(block.shape, block.dtype),
            pltpu.SemaphoreType.DMA((4,)),
            pltpu.SemaphoreType.DMA((1,)),
        ],
        compiler_params=pltpu.CompilerParams(vmem_limit_bytes=VMEM_LIMIT),
        cost_estimate=pl.CostEstimate(flops=0, bytes_accessed=2 * math.prod(tiles.shape), transcendentals=0),
    )(count, in_hbm(block), in_hbm(tiles))


def products(turned_ref, tiles_ref, group_starts):
    slots, width, extent = tiles_ref.shape
    half = turned_ref.shape[0] // 2
    step = SUB * width
    lhs = jnp.concatenate(
        [
            turned_ref[pl.ds(pl.multiple_of(first + at, SUB), SUB), :]
            for first in (0, half)
            for at in group_starts
        ],
        axis=0,
    )
    for at in range(extent // step):
        rhs = tiles_ref[:, :, at * step:(at + 1) * step].reshape(slots * width, step)
        yield at, jnp.dot(lhs, rhs, preferred_element_type=jnp.float32)


def arrange(chunks, groups, width, place, outs):
    row_at = lax.broadcasted_iota(jnp.int32, (SUB * SUB, SUB * SUB), 0)
    col_at = lax.broadcasted_iota(jnp.int32, (SUB * SUB, SUB * SUB), 1)
    bits = SUB.bit_length() - 1
    swap = (col_at == ((row_at & (SUB - 1)) << bits) + (row_at >> bits)).astype(jnp.bfloat16)
    low = lax.broadcasted_iota(jnp.int32, (SUB, LANES), 1) < width
    sides = []
    for at, acc in chunks:
        for s in range(groups):
            per_mu = []
            for q in range(acc.shape[1] // LANES):
                a = acc[s * SUB:(s + 1) * SUB, q * LANES:(q + 1) * LANES]
                b = acc[(groups + s) * SUB:(groups + s + 1) * SUB, q * LANES:(q + 1) * LANES]
                per_mu.append(jnp.where(low, a, pltpu.roll(b, width, 1)).astype(jnp.bfloat16))
                per_mu.append(jnp.where(low, pltpu.roll(a, width, 1), b).astype(jnp.bfloat16))
            sides.append((at, s, jnp.concatenate(per_mu, axis=0)))
    moved = jnp.dot(
        swap, jnp.concatenate([side for _, _, side in sides], axis=1), preferred_element_type=jnp.float32
    ).astype(jnp.bfloat16)
    for n, (at, s, _) in enumerate(sides):
        for k in range(SUB):
            which, part, col = place(s, k)
            outs[which][part, at * SUB:(at + 1) * SUB, col * LANES:(col + 1) * LANES] = moved[
                k * SUB:(k + 1) * SUB, n * LANES:(n + 1) * LANES
            ]


def multiply(turned_ref, tiles_ref, group_starts, place, outs):
    chunks = list(products(turned_ref, tiles_ref, group_starts))
    arrange(chunks, len(group_starts), tiles_ref.shape[1], place, outs)


def arrange_kernel(width, rows_ref, out_ref):
    step = SUB * width
    chunks = [
        (at, rows_ref[:, at * step:(at + 1) * step].astype(jnp.float32)) for at in range(rows_ref.shape[1] // step)
    ]
    arrange(chunks, 1, width, lambda s, k: (0, 0, k), [out_ref])


def arranged(rows, width):
    made = rows.shape[0] * rows.shape[1] // width
    return pl.pallas_call(
        functools.partial(arrange_kernel, width),
        out_shape=jax.ShapeDtypeStruct((1, width, made), rows.dtype),
        in_specs=[pl.BlockSpec(memory_space=pltpu.VMEM)],
        out_specs=pl.BlockSpec(memory_space=pltpu.VMEM),
        compiler_params=pltpu.CompilerParams(vmem_limit_bytes=VMEM_LIMIT),
        cost_estimate=pl.CostEstimate(
            flops=2 * SUB * SUB * width * made, bytes_accessed=4 * width * made, transcendentals=0
        ),
    )(rows)


def first_kernel(group_starts, place, n_parts, plain, block_ref, tiles_ref, *refs):
    parts, (full_ref, turned_ref, *outs), picked = refs[:n_parts], refs[n_parts:-1], refs[-1]
    slots, width, _ = tiles_ref.shape
    depth = parts[0].shape[0]
    me = lax.axis_index("rep") if n_parts > 1 else 0
    for k in range(n_parts):
        full_ref[pl.ds(pl.multiple_of((me ^ k) * depth, depth), depth), :] = parts[k][...]
    for t in range(slots):
        row = pl.multiple_of(jnp.maximum(block_ref[0, t], 0) * width, width)
        rows = full_ref[pl.ds(row, width), :]
        picked[t * width:(t + 1) * width, :] = jnp.where(block_ref[0, t] >= 0, rows, jnp.zeros_like(rows))
    turned_ref[...] = picked[...].T
    if plain:
        for at, acc in products(turned_ref, tiles_ref, group_starts()):
            step = acc.shape[1]
            outs[0][:, at * step:(at + 1) * step] = acc.astype(jnp.bfloat16)
    else:
        multiply(turned_ref, tiles_ref, group_starts(), place, outs)


def next_kernel(group_starts, place, turned_ref, tiles_ref, skipped, *outs):
    multiply(turned_ref, tiles_ref, group_starts(), place, outs)


def contract_cost(tiles, norb, out_shapes):
    slots, width, extent = tiles.shape
    made = sum(math.prod(shape) for shape in out_shapes)
    return pl.CostEstimate(
        flops=2 * slots * width * made, bytes_accessed=2 * slots * width * extent + 2 * made, transcendentals=0
    )


def contract_first(group_starts, place, out_shapes, block, tiles, parts, plain=False):
    slots, width, _ = tiles.shape
    depth, norb = parts[0].shape
    shapes = [(depth * len(parts), norb), (norb, slots * width)] + out_shapes
    full, turned, *made = pl.pallas_call(
        functools.partial(first_kernel, group_starts, place, len(parts), plain),
        out_shape=[jax.ShapeDtypeStruct(shape, jnp.bfloat16) for shape in shapes],
        in_specs=[pl.BlockSpec(memory_space=pltpu.VMEM)] * (2 + len(parts)),
        out_specs=[pl.BlockSpec(memory_space=pltpu.VMEM)] * len(shapes),
        scratch_shapes=[pltpu.VMEM((slots * width, norb), jnp.bfloat16)],
        compiler_params=pltpu.CompilerParams(vmem_limit_bytes=VMEM_LIMIT),
        cost_estimate=contract_cost(tiles, norb, out_shapes),
    )(block, tiles, *parts)
    return full, turned, made


def contract_next(group_starts, place, out_shapes, turned, tiles, after):
    return pl.pallas_call(
        functools.partial(next_kernel, group_starts, place),
        out_shape=[jax.ShapeDtypeStruct(shape, jnp.bfloat16) for shape in out_shapes],
        in_specs=[pl.BlockSpec(memory_space=pltpu.VMEM)] * 2 + [pl.BlockSpec(memory_space=pl.ANY)],
        out_specs=[pl.BlockSpec(memory_space=pltpu.VMEM)] * len(out_shapes),
        compiler_params=pltpu.CompilerParams(vmem_limit_bytes=VMEM_LIMIT),
        cost_estimate=contract_cost(tiles, turned.shape[0], out_shapes),
    )(turned, tiles, after)


def orbital_rows(orb_ref, width, ids):
    rows = [orb_ref[pl.ds(pl.multiple_of(b * width, width), width), :] for b in ids]
    return jnp.concatenate(rows, axis=0).T


def joined(refs, lanes=slice(None)):
    return jnp.concatenate([ref[:, :, lanes].reshape(-1, ref[:, :, lanes].shape[2]) for ref in refs], axis=0)


def fit_kernel(step, width, early_ids, late_ids, orb_ref, *refs):
    rows, (out_ref, *late_ref) = refs[:-1 - bool(late_ids)], refs[-1 - bool(late_ids):]
    turned = orbital_rows(orb_ref, width, early_ids())
    for at in range(out_ref.shape[1] // step):
        lanes = slice(at * step, (at + 1) * step)
        out_ref[:, lanes] = jnp.dot(turned, joined(rows, lanes), preferred_element_type=jnp.float32)
    if late_ids:
        late_ref[0][...] = orbital_rows(orb_ref, width, late_ids())


def fit(orbitals, early, n_late, early_ids, late_ids):
    width, cols = early[0].shape[1:]
    number = sum(each.shape[0] for each in early)
    norb = orbitals.shape[1]
    shapes = [jax.ShapeDtypeStruct((norb, cols), jnp.float32)]
    if n_late:
        shapes.append(jax.ShapeDtypeStruct((norb, n_late * width), jnp.bfloat16))
    return pl.pallas_call(
        functools.partial(fit_kernel, min(512, cols), width, early_ids, late_ids),
        out_shape=shapes,
        in_specs=[pl.BlockSpec(memory_space=pltpu.VMEM)] * (1 + len(early)),
        out_specs=[pl.BlockSpec(memory_space=pltpu.VMEM)] * len(shapes),
        compiler_params=pltpu.CompilerParams(vmem_limit_bytes=VMEM_LIMIT),
        cost_estimate=pl.CostEstimate(
            flops=2 * number * width * cols * norb,
            bytes_accessed=2 * number * width * cols + 4 * norb * cols,
            transcendentals=0,
        ),
    )(orbitals, *early)


def action_half(rows, fitted, mix_scale, half, width, ids, out_ref):
    offset = pl.multiple_of(half * (width // 2), width // 2)
    lhs = jnp.concatenate(
        [ref[b, pl.ds(offset, width // 2), :] for ref in rows for b in range(ref.shape[0])], axis=0
    )
    term = lax.dot_general(lhs, fitted, (((1,), (1,)), ((), ())), preferred_element_type=jnp.float32)
    term = (-mix_scale * term).reshape((-1,) + out_ref.shape[1:])
    for k, b in enumerate(ids):
        out_ref[b] = term[k]


def send_kernel(fit_scale, mix_scale, step, width, ids, n_early, n_late, fitted_ref, *refs):
    rows, late, (send_ref, out_ref) = refs[:n_early + n_late], refs[n_early:n_early + n_late], refs[-2:]
    cols = fitted_ref.shape[1]
    if late:
        turned = refs[n_early + n_late][...]
    for at in range(cols // step):
        lanes = slice(at * step, (at + 1) * step)
        total = fitted_ref[:, lanes]
        if late:
            total = total + jnp.dot(turned, joined(late, lanes), preferred_element_type=jnp.float32)
        out_ref[:, lanes] = (fit_scale * total).astype(jnp.bfloat16)
    core = lax.axis_index("rep") % 2
    action_half(rows, out_ref[...], mix_scale, 1 - core, width, ids(), send_ref)


def keep_kernel(mix_scale, width, ids, fitted_ref, *refs):
    core = lax.axis_index("rep") % 2
    action_half(refs[:-1], fitted_ref[...], mix_scale, core, width, ids(), refs[-1])


def action(fitted, early, late, ids, basis_rows, fit_scale, mix_scale):
    norb, cols = fitted[0].shape
    width = early[0].shape[1]
    blocks = basis_rows // width
    half = jax.ShapeDtypeStruct((blocks, width // 2, norb), jnp.float32)
    rows = list(early) + list(late)
    params = pltpu.CompilerParams(vmem_limit_bytes=VMEM_LIMIT)
    cost = pl.CostEstimate(
        flops=2 * blocks * width * cols * norb, bytes_accessed=2 * blocks * width * cols, transcendentals=0
    )
    send, columns = pl.pallas_call(
        functools.partial(
            send_kernel, fit_scale, mix_scale, min(512, cols), width, ids, len(early), len(late)
        ),
        out_shape=[half, jax.ShapeDtypeStruct((norb, cols), jnp.bfloat16)],
        in_specs=[pl.BlockSpec(memory_space=pltpu.VMEM)] * (len(fitted) + len(rows)),
        out_specs=[pl.BlockSpec(memory_space=pltpu.VMEM)] * 2,
        compiler_params=params,
        cost_estimate=cost,
    )(fitted[0], *rows, *fitted[1:])
    keep = pl.pallas_call(
        functools.partial(keep_kernel, mix_scale, width, ids),
        out_shape=half,
        in_specs=[pl.BlockSpec(memory_space=pltpu.VMEM)] * (1 + len(rows)),
        out_specs=pl.BlockSpec(memory_space=pltpu.VMEM),
        compiler_params=params,
        cost_estimate=cost,
    )(columns, *rows)
    return keep, send


def swapped(x, axis, k):
    return lax.ppermute(x, axis, [(i, i ^ k) for i in range(lax.axis_size(axis))])


def summed_blocks(blocks, axis):
    rows = blocks.shape[1]
    largest = jnp.max(jnp.abs(blocks), axis=1, keepdims=True)
    exponent = jnp.ceil(jnp.log2(jnp.maximum(largest, 1e-30))) - 14
    scaled = (blocks * jnp.exp2(-exponent)).astype(jnp.float16)
    tail = jnp.broadcast_to(exponent.astype(jnp.float16), (blocks.shape[0], 8, blocks.shape[2]))
    got = lax.all_to_all(jnp.concatenate([scaled, tail], axis=1), axis, 0, 0, tiled=True).astype(jnp.float32)
    return jnp.sum(got[:, :rows] * jnp.exp2(got[:, rows:rows + 1]), axis=0)


def per_device(orbitals, tiles, tile_block, tile_count):
    rep_size = lax.axis_size("rep")
    grid_size = lax.axis_size("grid")
    width = tiles.shape[3]
    depth, norb = orbitals.shape
    half = norb // 2
    cols = width * norb // grid_size
    basis_rows = depth * rep_size
    fit_scale = 1.0 / math.sqrt(basis_rows)
    mix_scale = 0.25 / math.sqrt(width * rep_size * norb)
    inside, block = load(tiles, tile_count, tile_block)
    per_part = half // grid_size
    if per_part == SUB and grid_size == 8 and rep_size == 4:
        near_size = grid_size // 2
        parts = [orbitals] + [swapped(orbitals, "rep", k) for k in range(1, rep_size)]

        def ids(ks):
            def blocks():
                me = lax.axis_index("grid")
                return [me ^ k for k in ks]

            return blocks

        def starts(ks):
            return lambda: [b * SUB for b in ids(ks)()]

        def own_output(s, k):
            return s, 0, k

        def shapes(ks):
            return [(1, width, cols)] * len(ks)

        waves, late_ks = [[6], [0, 2, 3, 1], [5, 4, 7]], [5, 4, 7]
        full, turned, made = contract_first(
            starts(waves[0]), None, [(2 * SUB, tiles.shape[4])], block, inside, parts, plain=True
        )
        sent = dict(zip(waves[0], made))
        for wave in waves[1:]:
            made = contract_next(starts(wave), own_output, shapes(wave), turned, inside, made[0])
            sent.update(zip(wave, made))
        received = {k: swapped(sent[k], "grid", k) if k else sent[k] for wave in waves for k in wave}
        received[waves[0][0]] = arranged(received[waves[0][0]], width)
        early_ks = [k for wave in waves for k in wave if k not in late_ks]
        early, late = [received[k] for k in early_ks], [received[k] for k in late_ks]
        early_ids, late_ids, all_ids = ids(early_ks), ids(late_ks), ids(early_ks + late_ks)
    else:
        def place(s, k):
            part, col = divmod(s * SUB + k, per_part)
            return 0, part, col

        parts = [lax.all_gather(orbitals, "rep", axis=0, tiled=True)]
        full, _, (sent,) = contract_first(
            lambda: list(range(0, half, SUB)), place, [(grid_size, width, cols)], block, inside, parts
        )
        early, late = [lax.all_to_all(sent, "grid", 0, 0, tiled=True)], []

        def early_ids():
            return list(range(grid_size))

        late_ids, all_ids = None, early_ids
    fitted = fit(full, early, len(late), early_ids, late_ids)
    part_keep, part_send = action(fitted, early, late, all_ids, basis_rows, fit_scale, mix_scale)
    pair = part_keep + swapped(part_send, "rep", 1)
    mine = summed_blocks(pair, "grid")
    if rep_size == 4:
        other, across = swapped(mine, "rep", 2), swapped(mine, "rep", 3)
        beside = swapped(mine, "rep", 1)
        own, theirs = mine + other, beside + across
        upper = lax.axis_index("rep") % 2 == 1
        return jnp.concatenate([jnp.where(upper, theirs, own), jnp.where(upper, own, theirs)], axis=0)
    every = lax.all_gather(mine, "rep", axis=0, tiled=False)
    return jnp.sum(every.reshape(rep_size // 2, 2, width // 2, norb), axis=0).reshape(width, norb)


def solution(mesh):
    in_specs = (
        P("rep", None),
        P("rep", "grid", None, None, None),
        P("rep", "grid", None),
        P("rep", "grid"),
    )
    return jax.shard_map(
        per_device, mesh=mesh, in_specs=in_specs, out_specs=P("grid", None), check_vma=False
    )
```

```python
import functools
import math

import jax
import jax.numpy as jnp
from jax import lax
from jax.experimental import pallas as pl
from jax.experimental.pallas import tpu as pltpu
from jax.sharding import PartitionSpec as P

LANES = 128
SUB = 16
VMEM_LIMIT = 24 * 1024 * 1024


def load_kernel(count_ref, block_hbm, tiles_hbm, out_ref, live_ref, block, sems, block_sem):
    chunks = sems.shape[0]
    step = out_ref.shape[2] // chunks
    copies = [
        pltpu.make_async_copy(
            tiles_hbm.at[0, 0, :, :, pl.ds(at * step, step)], out_ref.at[:, :, pl.ds(at * step, step)], sems.at[at]
        )
        for at in range(chunks)
    ]
    block_copy = pltpu.make_async_copy(block_hbm, block, block_sem.at[0])
    block_copy.start()
    for each in copies:
        each.start()
    block_copy.wait()
    slot = lax.broadcasted_iota(jnp.int32, live_ref.shape, 1)
    live_ref[...] = jnp.where(slot < count_ref[0, 0], block[0], -1)
    for each in copies:
        each.wait()


def in_hbm(x):
    return pltpu.with_memory_space_constraint(x, pltpu.HBM)


def load(tiles, count, block):
    return pl.pallas_call(
        load_kernel,
        out_shape=[
            jax.ShapeDtypeStruct(tiles.shape[2:], tiles.dtype),
            jax.ShapeDtypeStruct(block.shape[1:], block.dtype),
        ],
        in_specs=[
            pl.BlockSpec(memory_space=pltpu.SMEM),
            pl.BlockSpec(memory_space=pltpu.HBM),
            pl.BlockSpec(memory_space=pltpu.HBM),
        ],
        out_specs=[pl.BlockSpec(memory_space=pltpu.VMEM)] * 2,
        scratch_shapes=[
            pltpu.VMEM(block.shape, block.dtype),
            pltpu.SemaphoreType.DMA((4,)),
            pltpu.SemaphoreType.DMA((1,)),
        ],
        compiler_params=pltpu.CompilerParams(vmem_limit_bytes=VMEM_LIMIT),
        cost_estimate=pl.CostEstimate(flops=0, bytes_accessed=2 * math.prod(tiles.shape), transcendentals=0),
    )(count, in_hbm(block), in_hbm(tiles))


def products(turned_ref, tiles_ref, group_starts):
    slots, width, extent = tiles_ref.shape
    half = turned_ref.shape[0] // 2
    step = SUB * width
    lhs = jnp.concatenate(
        [
            turned_ref[pl.ds(pl.multiple_of(first + at, SUB), SUB), :]
            for first in (0, half)
            for at in group_starts
        ],
        axis=0,
    )
    for at in range(extent // step):
        rhs = tiles_ref[:, :, at * step:(at + 1) * step].reshape(slots * width, step)
        yield at, jnp.dot(lhs, rhs, preferred_element_type=jnp.float32)


def arrange(chunks, groups, width, place, outs):
    row_at = lax.broadcasted_iota(jnp.int32, (SUB * SUB, SUB * SUB), 0)
    col_at = lax.broadcasted_iota(jnp.int32, (SUB * SUB, SUB * SUB), 1)
    bits = SUB.bit_length() - 1
    swap = (col_at == ((row_at & (SUB - 1)) << bits) + (row_at >> bits)).astype(jnp.bfloat16)
    low = lax.broadcasted_iota(jnp.int32, (SUB, LANES), 1) < width
    sides = []
    for at, acc in chunks:
        for s in range(groups):
            per_mu = []
            for q in range(acc.shape[1] // LANES):
                a = acc[s * SUB:(s + 1) * SUB, q * LANES:(q + 1) * LANES]
                b = acc[(groups + s) * SUB:(groups + s + 1) * SUB, q * LANES:(q + 1) * LANES]
                per_mu.append(jnp.where(low, a, pltpu.roll(b, width, 1)).astype(jnp.bfloat16))
                per_mu.append(jnp.where(low, pltpu.roll(a, width, 1), b).astype(jnp.bfloat16))
            sides.append((at, s, jnp.concatenate(per_mu, axis=0)))
    moved = jnp.dot(
        swap, jnp.concatenate([side for _, _, side in sides], axis=1), preferred_element_type=jnp.float32
    ).astype(jnp.bfloat16)
    for n, (at, s, _) in enumerate(sides):
        for k in range(SUB):
            which, part, col = place(s, k)
            outs[which][part, at * SUB:(at + 1) * SUB, col * LANES:(col + 1) * LANES] = moved[
                k * SUB:(k + 1) * SUB, n * LANES:(n + 1) * LANES
            ]


def multiply(turned_ref, tiles_ref, group_starts, place, outs):
    chunks = list(products(turned_ref, tiles_ref, group_starts))
    arrange(chunks, len(group_starts), tiles_ref.shape[1], place, outs)


def arrange_kernel(width, rows_ref, out_ref):
    step = SUB * width
    chunks = [
        (at, rows_ref[:, at * step:(at + 1) * step].astype(jnp.float32)) for at in range(rows_ref.shape[1] // step)
    ]
    arrange(chunks, 1, width, lambda s, k: (0, 0, k), [out_ref])


def arranged(rows, width):
    made = rows.shape[0] * rows.shape[1] // width
    return pl.pallas_call(
        functools.partial(arrange_kernel, width),
        out_shape=jax.ShapeDtypeStruct((1, width, made), rows.dtype),
        in_specs=[pl.BlockSpec(memory_space=pltpu.VMEM)],
        out_specs=pl.BlockSpec(memory_space=pltpu.VMEM),
        compiler_params=pltpu.CompilerParams(vmem_limit_bytes=VMEM_LIMIT),
        cost_estimate=pl.CostEstimate(
            flops=2 * SUB * SUB * width * made, bytes_accessed=4 * width * made, transcendentals=0
        ),
    )(rows)


def first_kernel(group_starts, place, n_parts, plain, block_ref, tiles_ref, *refs):
    parts, (full_ref, turned_ref, *outs), picked = refs[:n_parts], refs[n_parts:-1], refs[-1]
    slots, width, _ = tiles_ref.shape
    depth = parts[0].shape[0]
    me = lax.axis_index("rep") if n_parts > 1 else 0
    for k in range(n_parts):
        full_ref[pl.ds(pl.multiple_of((me ^ k) * depth, depth), depth), :] = parts[k][...]
    for t in range(slots):
        row = pl.multiple_of(jnp.maximum(block_ref[0, t], 0) * width, width)
        rows = full_ref[pl.ds(row, width), :]
        picked[t * width:(t + 1) * width, :] = jnp.where(block_ref[0, t] >= 0, rows, jnp.zeros_like(rows))
    turned_ref[...] = picked[...].T
    if plain:
        for at, acc in products(turned_ref, tiles_ref, group_starts()):
            step = acc.shape[1]
            outs[0][:, at * step:(at + 1) * step] = acc.astype(jnp.bfloat16)
    else:
        multiply(turned_ref, tiles_ref, group_starts(), place, outs)


def next_kernel(group_starts, place, turned_ref, tiles_ref, skipped, *outs):
    multiply(turned_ref, tiles_ref, group_starts(), place, outs)


def contract_cost(tiles, norb, out_shapes):
    slots, width, extent = tiles.shape
    made = sum(math.prod(shape) for shape in out_shapes)
    return pl.CostEstimate(
        flops=2 * slots * width * made, bytes_accessed=2 * slots * width * extent + 2 * made, transcendentals=0
    )


def contract_first(group_starts, place, out_shapes, block, tiles, parts, plain=False):
    slots, width, _ = tiles.shape
    depth, norb = parts[0].shape
    shapes = [(depth * len(parts), norb), (norb, slots * width)] + out_shapes
    full, turned, *made = pl.pallas_call(
        functools.partial(first_kernel, group_starts, place, len(parts), plain),
        out_shape=[jax.ShapeDtypeStruct(shape, jnp.bfloat16) for shape in shapes],
        in_specs=[pl.BlockSpec(memory_space=pltpu.VMEM)] * (2 + len(parts)),
        out_specs=[pl.BlockSpec(memory_space=pltpu.VMEM)] * len(shapes),
        scratch_shapes=[pltpu.VMEM((slots * width, norb), jnp.bfloat16)],
        compiler_params=pltpu.CompilerParams(vmem_limit_bytes=VMEM_LIMIT),
        cost_estimate=contract_cost(tiles, norb, out_shapes),
    )(block, tiles, *parts)
    return full, turned, made


def contract_next(group_starts, place, out_shapes, turned, tiles, after):
    return pl.pallas_call(
        functools.partial(next_kernel, group_starts, place),
        out_shape=[jax.ShapeDtypeStruct(shape, jnp.bfloat16) for shape in out_shapes],
        in_specs=[pl.BlockSpec(memory_space=pltpu.VMEM)] * 2 + [pl.BlockSpec(memory_space=pl.ANY)],
        out_specs=[pl.BlockSpec(memory_space=pltpu.VMEM)] * len(out_shapes),
        compiler_params=pltpu.CompilerParams(vmem_limit_bytes=VMEM_LIMIT),
        cost_estimate=contract_cost(tiles, turned.shape[0], out_shapes),
    )(turned, tiles, after)


def orbital_rows(orb_ref, width, ids):
    rows = [orb_ref[pl.ds(pl.multiple_of(b * width, width), width), :] for b in ids]
    return jnp.concatenate(rows, axis=0).T


def joined(refs, lanes=slice(None)):
    return jnp.concatenate([ref[:, :, lanes].reshape(-1, ref[:, :, lanes].shape[2]) for ref in refs], axis=0)


def fit_kernel(step, width, early_ids, late_ids, orb_ref, *refs):
    rows, (out_ref, *late_ref) = refs[:-1 - bool(late_ids)], refs[-1 - bool(late_ids):]
    turned = orbital_rows(orb_ref, width, early_ids())
    for at in range(out_ref.shape[1] // step):
        lanes = slice(at * step, (at + 1) * step)
        out_ref[:, lanes] = jnp.dot(turned, joined(rows, lanes), preferred_element_type=jnp.float32)
    if late_ids:
        late_ref[0][...] = orbital_rows(orb_ref, width, late_ids())


def fit(orbitals, early, n_late, early_ids, late_ids):
    width, cols = early[0].shape[1:]
    number = sum(each.shape[0] for each in early)
    norb = orbitals.shape[1]
    shapes = [jax.ShapeDtypeStruct((norb, cols), jnp.float32)]
    if n_late:
        shapes.append(jax.ShapeDtypeStruct((norb, n_late * width), jnp.bfloat16))
    return pl.pallas_call(
        functools.partial(fit_kernel, min(512, cols), width, early_ids, late_ids),
        out_shape=shapes,
        in_specs=[pl.BlockSpec(memory_space=pltpu.VMEM)] * (1 + len(early)),
        out_specs=[pl.BlockSpec(memory_space=pltpu.VMEM)] * len(shapes),
        compiler_params=pltpu.CompilerParams(vmem_limit_bytes=VMEM_LIMIT),
        cost_estimate=pl.CostEstimate(
            flops=2 * number * width * cols * norb,
            bytes_accessed=2 * number * width * cols + 4 * norb * cols,
            transcendentals=0,
        ),
    )(orbitals, *early)


def action_half(rows, fitted, mix_scale, half, width, ids, out_ref):
    offset = pl.multiple_of(half * (width // 2), width // 2)
    lhs = jnp.concatenate(
        [ref[b, pl.ds(offset, width // 2), :] for ref in rows for b in range(ref.shape[0])], axis=0
    )
    term = lax.dot_general(lhs, fitted, (((1,), (1,)), ((), ())), preferred_element_type=jnp.float32)
    term = (-mix_scale * term).reshape((-1,) + out_ref.shape[1:])
    for k, b in enumerate(ids):
        out_ref[b] = term[k]


def send_kernel(fit_scale, mix_scale, step, width, ids, n_early, n_late, fitted_ref, *refs):
    rows, late, (send_ref, out_ref) = refs[:n_early + n_late], refs[n_early:n_early + n_late], refs[-2:]
    cols = fitted_ref.shape[1]
    if late:
        turned = refs[n_early + n_late][...]
    for at in range(cols // step):
        lanes = slice(at * step, (at + 1) * step)
        total = fitted_ref[:, lanes]
        if late:
            total = total + jnp.dot(turned, joined(late, lanes), preferred_element_type=jnp.float32)
        out_ref[:, lanes] = (fit_scale * total).astype(jnp.bfloat16)
    core = lax.axis_index("rep") % 2
    action_half(rows, out_ref[...], mix_scale, 1 - core, width, ids(), send_ref)


def keep_kernel(mix_scale, width, ids, fitted_ref, *refs):
    core = lax.axis_index("rep") % 2
    action_half(refs[:-1], fitted_ref[...], mix_scale, core, width, ids(), refs[-1])


def action(fitted, early, late, ids, basis_rows, fit_scale, mix_scale):
    norb, cols = fitted[0].shape
    width = early[0].shape[1]
    blocks = basis_rows // width
    half = jax.ShapeDtypeStruct((blocks, width // 2, norb), jnp.float32)
    rows = list(early) + list(late)
    params = pltpu.CompilerParams(vmem_limit_bytes=VMEM_LIMIT)
    cost = pl.CostEstimate(
        flops=2 * blocks * width * cols * norb, bytes_accessed=2 * blocks * width * cols, transcendentals=0
    )
    send, columns = pl.pallas_call(
        functools.partial(
            send_kernel, fit_scale, mix_scale, cols, width, ids, len(early), len(late)
        ),
        out_shape=[half, jax.ShapeDtypeStruct((norb, cols), jnp.bfloat16)],
        in_specs=[pl.BlockSpec(memory_space=pltpu.VMEM)] * (len(fitted) + len(rows)),
        out_specs=[pl.BlockSpec(memory_space=pltpu.VMEM)] * 2,
        compiler_params=params,
        cost_estimate=cost,
    )(fitted[0], *rows, *fitted[1:])
    keep = pl.pallas_call(
        functools.partial(keep_kernel, mix_scale, width, ids),
        out_shape=half,
        in_specs=[pl.BlockSpec(memory_space=pltpu.VMEM)] * (1 + len(rows)),
        out_specs=pl.BlockSpec(memory_space=pltpu.VMEM),
        compiler_params=params,
        cost_estimate=cost,
    )(columns, *rows)
    return keep, send


def swapped(x, axis, k):
    return lax.ppermute(x, axis, [(i, i ^ k) for i in range(lax.axis_size(axis))])


def summed_blocks(blocks, axis):
    rows = blocks.shape[1]
    largest = jnp.max(jnp.abs(blocks), axis=1, keepdims=True)
    exponent = jnp.ceil(jnp.log2(jnp.maximum(largest, 1e-30))) - 14
    scaled = (blocks * jnp.exp2(-exponent)).astype(jnp.float16)
    tail = jnp.broadcast_to(exponent.astype(jnp.float16), (blocks.shape[0], 8, blocks.shape[2]))
    got = lax.all_to_all(jnp.concatenate([scaled, tail], axis=1), axis, 0, 0, tiled=True).astype(jnp.float32)
    return jnp.sum(got[:, :rows] * jnp.exp2(got[:, rows:rows + 1]), axis=0)


def per_device(orbitals, tiles, tile_block, tile_count):
    rep_size = lax.axis_size("rep")
    grid_size = lax.axis_size("grid")
    width = tiles.shape[3]
    depth, norb = orbitals.shape
    half = norb // 2
    cols = width * norb // grid_size
    basis_rows = depth * rep_size
    fit_scale = 1.0 / math.sqrt(basis_rows)
    mix_scale = 0.25 / math.sqrt(width * rep_size * norb)
    inside, block = load(tiles, tile_count, tile_block)
    per_part = half // grid_size
    if per_part == SUB and grid_size == 8 and rep_size == 4:
        near_size = grid_size // 2
        parts = [orbitals] + [swapped(orbitals, "rep", k) for k in range(1, rep_size)]

        def ids(ks):
            def blocks():
                me = lax.axis_index("grid")
                return [me ^ k for k in ks]

            return blocks

        def starts(ks):
            return lambda: [b * SUB for b in ids(ks)()]

        def own_output(s, k):
            return s, 0, k

        def shapes(ks):
            return [(1, width, cols)] * len(ks)

        waves, late_ks = [[6], [0, 2, 3, 1], [5, 4, 7]], [5, 4, 7]
        full, turned, made = contract_first(
            starts(waves[0]), None, [(2 * SUB, tiles.shape[4])], block, inside, parts, plain=True
        )
        sent = dict(zip(waves[0], made))
        for wave in waves[1:]:
            made = contract_next(starts(wave), own_output, shapes(wave), turned, inside, made[0])
            sent.update(zip(wave, made))
        received = {k: swapped(sent[k], "grid", k) if k else sent[k] for wave in waves for k in wave}
        received[waves[0][0]] = arranged(received[waves[0][0]], width)
        early_ks = [k for wave in waves for k in wave if k not in late_ks]
        early, late = [received[k] for k in early_ks], [received[k] for k in late_ks]
        early_ids, late_ids, all_ids = ids(early_ks), ids(late_ks), ids(early_ks + late_ks)
    else:
        def place(s, k):
            part, col = divmod(s * SUB + k, per_part)
            return 0, part, col

        parts = [lax.all_gather(orbitals, "rep", axis=0, tiled=True)]
        full, _, (sent,) = contract_first(
            lambda: list(range(0, half, SUB)), place, [(grid_size, width, cols)], block, inside, parts
        )
        early, late = [lax.all_to_all(sent, "grid", 0, 0, tiled=True)], []

        def early_ids():
            return list(range(grid_size))

        late_ids, all_ids = None, early_ids
    fitted = fit(full, early, len(late), early_ids, late_ids)
    part_keep, part_send = action(fitted, early, late, all_ids, basis_rows, fit_scale, mix_scale)
    pair = part_keep + swapped(part_send, "rep", 1)
    mine = summed_blocks(pair, "grid")
    if rep_size == 4:
        other, across = swapped(mine, "rep", 2), swapped(mine, "rep", 3)
        beside = swapped(mine, "rep", 1)
        own, theirs = mine + other, beside + across
        upper = lax.axis_index("rep") % 2 == 1
        return jnp.concatenate([jnp.where(upper, theirs, own), jnp.where(upper, own, theirs)], axis=0)
    every = lax.all_gather(mine, "rep", axis=0, tiled=False)
    return jnp.sum(every.reshape(rep_size // 2, 2, width // 2, norb), axis=0).reshape(width, norb)


def solution(mesh):
    in_specs = (
        P("rep", None),
        P("rep", "grid", None, None, None),
        P("rep", "grid", None),
        P("rep", "grid"),
    )
    return jax.shard_map(
        per_device, mesh=mesh, in_specs=in_specs, out_specs=P("grid", None), check_vma=False
    )
```

```python
import functools
import math

import jax
import jax.numpy as jnp
from jax import lax
from jax.experimental import pallas as pl
from jax.experimental.pallas import tpu as pltpu
from jax.sharding import PartitionSpec as P

LANES = 128
SUB = 16
VMEM_LIMIT = 24 * 1024 * 1024


def load_kernel(count_ref, block_hbm, tiles_hbm, out_ref, live_ref, block, sems, block_sem):
    chunks = sems.shape[0]
    step = out_ref.shape[2] // chunks
    copies = [
        pltpu.make_async_copy(
            tiles_hbm.at[0, 0, :, :, pl.ds(at * step, step)], out_ref.at[:, :, pl.ds(at * step, step)], sems.at[at]
        )
        for at in range(chunks)
    ]
    block_copy = pltpu.make_async_copy(block_hbm, block, block_sem.at[0])
    block_copy.start()
    for each in copies:
        each.start()
    block_copy.wait()
    slot = lax.broadcasted_iota(jnp.int32, live_ref.shape, 1)
    live_ref[...] = jnp.where(slot < count_ref[0, 0], block[0], -1)
    for each in copies:
        each.wait()


def in_hbm(x):
    return pltpu.with_memory_space_constraint(x, pltpu.HBM)


def load(tiles, count, block):
    return pl.pallas_call(
        load_kernel,
        out_shape=[
            jax.ShapeDtypeStruct(tiles.shape[2:], tiles.dtype),
            jax.ShapeDtypeStruct(block.shape[1:], block.dtype),
        ],
        in_specs=[
            pl.BlockSpec(memory_space=pltpu.SMEM),
            pl.BlockSpec(memory_space=pltpu.HBM),
            pl.BlockSpec(memory_space=pltpu.HBM),
        ],
        out_specs=[pl.BlockSpec(memory_space=pltpu.VMEM)] * 2,
        scratch_shapes=[
            pltpu.VMEM(block.shape, block.dtype),
            pltpu.SemaphoreType.DMA((4,)),
            pltpu.SemaphoreType.DMA((1,)),
        ],
        compiler_params=pltpu.CompilerParams(vmem_limit_bytes=VMEM_LIMIT),
        cost_estimate=pl.CostEstimate(flops=0, bytes_accessed=2 * math.prod(tiles.shape), transcendentals=0),
    )(count, in_hbm(block), in_hbm(tiles))


def products(turned_ref, tiles_ref, group_starts):
    slots, width, extent = tiles_ref.shape
    half = turned_ref.shape[0] // 2
    step = SUB * width
    lhs = jnp.concatenate(
        [
            turned_ref[pl.ds(pl.multiple_of(first + at, SUB), SUB), :]
            for first in (0, half)
            for at in group_starts
        ],
        axis=0,
    )
    for at in range(extent // step):
        rhs = tiles_ref[:, :, at * step:(at + 1) * step].reshape(slots * width, step)
        yield at, jnp.dot(lhs, rhs, preferred_element_type=jnp.float32)


def arrange(chunks, groups, width, place, outs):
    row_at = lax.broadcasted_iota(jnp.int32, (SUB * SUB, SUB * SUB), 0)
    col_at = lax.broadcasted_iota(jnp.int32, (SUB * SUB, SUB * SUB), 1)
    bits = SUB.bit_length() - 1
    swap = (col_at == ((row_at & (SUB - 1)) << bits) + (row_at >> bits)).astype(jnp.bfloat16)
    low = lax.broadcasted_iota(jnp.int32, (SUB, LANES), 1) < width
    sides = []
    for at, acc in chunks:
        for s in range(groups):
            per_mu = []
            for q in range(acc.shape[1] // LANES):
                a = acc[s * SUB:(s + 1) * SUB, q * LANES:(q + 1) * LANES]
                b = acc[(groups + s) * SUB:(groups + s + 1) * SUB, q * LANES:(q + 1) * LANES]
                per_mu.append(jnp.where(low, a, pltpu.roll(b, width, 1)).astype(jnp.bfloat16))
                per_mu.append(jnp.where(low, pltpu.roll(a, width, 1), b).astype(jnp.bfloat16))
            sides.append((at, s, jnp.concatenate(per_mu, axis=0)))
    moved = jnp.dot(
        swap, jnp.concatenate([side for _, _, side in sides], axis=1), preferred_element_type=jnp.float32
    ).astype(jnp.bfloat16)
    for n, (at, s, _) in enumerate(sides):
        for k in range(SUB):
            which, part, col = place(s, k)
            outs[which][part, at * SUB:(at + 1) * SUB, col * LANES:(col + 1) * LANES] = moved[
                k * SUB:(k + 1) * SUB, n * LANES:(n + 1) * LANES
            ]


def multiply(turned_ref, tiles_ref, group_starts, place, outs):
    chunks = list(products(turned_ref, tiles_ref, group_starts))
    arrange(chunks, len(group_starts), tiles_ref.shape[1], place, outs)


def arrange_kernel(width, rows_ref, out_ref):
    step = SUB * width
    chunks = [
        (at, rows_ref[:, at * step:(at + 1) * step].astype(jnp.float32)) for at in range(rows_ref.shape[1] // step)
    ]
    arrange(chunks, 1, width, lambda s, k: (0, 0, k), [out_ref])


def arranged(rows, width):
    made = rows.shape[0] * rows.shape[1] // width
    return pl.pallas_call(
        functools.partial(arrange_kernel, width),
        out_shape=jax.ShapeDtypeStruct((1, width, made), rows.dtype),
        in_specs=[pl.BlockSpec(memory_space=pltpu.VMEM)],
        out_specs=pl.BlockSpec(memory_space=pltpu.VMEM),
        compiler_params=pltpu.CompilerParams(vmem_limit_bytes=VMEM_LIMIT),
        cost_estimate=pl.CostEstimate(
            flops=2 * SUB * SUB * width * made, bytes_accessed=4 * width * made, transcendentals=0
        ),
    )(rows)


def first_kernel(group_starts, place, n_parts, plain, block_ref, tiles_ref, *refs):
    parts, (full_ref, turned_ref, *outs), picked = refs[:n_parts], refs[n_parts:-1], refs[-1]
    slots, width, _ = tiles_ref.shape
    depth = parts[0].shape[0]
    me = lax.axis_index("rep") if n_parts > 1 else 0
    for k in range(n_parts):
        full_ref[pl.ds(pl.multiple_of((me ^ k) * depth, depth), depth), :] = parts[k][...]
    for t in range(slots):
        row = pl.multiple_of(jnp.maximum(block_ref[0, t], 0) * width, width)
        rows = full_ref[pl.ds(row, width), :]
        picked[t * width:(t + 1) * width, :] = jnp.where(block_ref[0, t] >= 0, rows, jnp.zeros_like(rows))
    turned_ref[...] = picked[...].T
    if plain:
        for at, acc in products(turned_ref, tiles_ref, group_starts()):
            step = acc.shape[1]
            outs[0][:, at * step:(at + 1) * step] = acc.astype(jnp.bfloat16)
    else:
        multiply(turned_ref, tiles_ref, group_starts(), place, outs)


def next_kernel(group_starts, place, turned_ref, tiles_ref, skipped, *outs):
    multiply(turned_ref, tiles_ref, group_starts(), place, outs)


def contract_cost(tiles, norb, out_shapes):
    slots, width, extent = tiles.shape
    made = sum(math.prod(shape) for shape in out_shapes)
    return pl.CostEstimate(
        flops=2 * slots * width * made, bytes_accessed=2 * slots * width * extent + 2 * made, transcendentals=0
    )


def contract_first(group_starts, place, out_shapes, block, tiles, parts, plain=False):
    slots, width, _ = tiles.shape
    depth, norb = parts[0].shape
    shapes = [(depth * len(parts), norb), (norb, slots * width)] + out_shapes
    full, turned, *made = pl.pallas_call(
        functools.partial(first_kernel, group_starts, place, len(parts), plain),
        out_shape=[jax.ShapeDtypeStruct(shape, jnp.bfloat16) for shape in shapes],
        in_specs=[pl.BlockSpec(memory_space=pltpu.VMEM)] * (2 + len(parts)),
        out_specs=[pl.BlockSpec(memory_space=pltpu.VMEM)] * len(shapes),
        scratch_shapes=[pltpu.VMEM((slots * width, norb), jnp.bfloat16)],
        compiler_params=pltpu.CompilerParams(vmem_limit_bytes=VMEM_LIMIT),
        cost_estimate=contract_cost(tiles, norb, out_shapes),
    )(block, tiles, *parts)
    return full, turned, made


def contract_next(group_starts, place, out_shapes, turned, tiles, after):
    return pl.pallas_call(
        functools.partial(next_kernel, group_starts, place),
        out_shape=[jax.ShapeDtypeStruct(shape, jnp.bfloat16) for shape in out_shapes],
        in_specs=[pl.BlockSpec(memory_space=pltpu.VMEM)] * 2 + [pl.BlockSpec(memory_space=pl.ANY)],
        out_specs=[pl.BlockSpec(memory_space=pltpu.VMEM)] * len(out_shapes),
        compiler_params=pltpu.CompilerParams(vmem_limit_bytes=VMEM_LIMIT),
        cost_estimate=contract_cost(tiles, turned.shape[0], out_shapes),
    )(turned, tiles, after)


def orbital_rows(orb_ref, width, ids):
    rows = [orb_ref[pl.ds(pl.multiple_of(b * width, width), width), :] for b in ids]
    return jnp.concatenate(rows, axis=0).T


def joined(refs, lanes=slice(None)):
    return jnp.concatenate([ref[:, :, lanes].reshape(-1, ref[:, :, lanes].shape[2]) for ref in refs], axis=0)


def fit_kernel(step, width, early_ids, late_ids, orb_ref, *refs):
    rows, (out_ref, *late_ref) = refs[:-1 - bool(late_ids)], refs[-1 - bool(late_ids):]
    turned = orbital_rows(orb_ref, width, early_ids())
    for at in range(out_ref.shape[1] // step):
        lanes = slice(at * step, (at + 1) * step)
        out_ref[:, lanes] = jnp.dot(turned, joined(rows, lanes), preferred_element_type=jnp.float32)
    if late_ids:
        late_ref[0][...] = orbital_rows(orb_ref, width, late_ids())


def fit(orbitals, early, n_late, early_ids, late_ids):
    width, cols = early[0].shape[1:]
    number = sum(each.shape[0] for each in early)
    norb = orbitals.shape[1]
    shapes = [jax.ShapeDtypeStruct((norb, cols), jnp.float32)]
    if n_late:
        shapes.append(jax.ShapeDtypeStruct((norb, n_late * width), jnp.bfloat16))
    return pl.pallas_call(
        functools.partial(fit_kernel, min(512, cols), width, early_ids, late_ids),
        out_shape=shapes,
        in_specs=[pl.BlockSpec(memory_space=pltpu.VMEM)] * (1 + len(early)),
        out_specs=[pl.BlockSpec(memory_space=pltpu.VMEM)] * len(shapes),
        compiler_params=pltpu.CompilerParams(vmem_limit_bytes=VMEM_LIMIT),
        cost_estimate=pl.CostEstimate(
            flops=2 * number * width * cols * norb,
            bytes_accessed=2 * number * width * cols + 4 * norb * cols,
            transcendentals=0,
        ),
    )(orbitals, *early)


def action_half(rows, fitted, mix_scale, half, width, ids, out_ref):
    offset = pl.multiple_of(half * (width // 2), width // 2)
    lhs = jnp.concatenate(
        [ref[b, pl.ds(offset, width // 2), :] for ref in rows for b in range(ref.shape[0])], axis=0
    )
    term = lax.dot_general(lhs, fitted, (((1,), (1,)), ((), ())), preferred_element_type=jnp.float32)
    term = (-mix_scale * term).reshape((-1,) + out_ref.shape[1:])
    for k, b in enumerate(ids):
        out_ref[b] = term[k]


def send_kernel(fit_scale, mix_scale, step, width, ids, n_early, n_late, fitted_ref, *refs):
    rows, late, (send_ref, out_ref) = refs[:n_early + n_late], refs[n_early:n_early + n_late], refs[-2:]
    cols = fitted_ref.shape[1]
    if late:
        turned = refs[n_early + n_late][...]
    for at in range(cols // step):
        lanes = slice(at * step, (at + 1) * step)
        total = fitted_ref[:, lanes]
        if late:
            total = total + jnp.dot(turned, joined(late, lanes), preferred_element_type=jnp.float32)
        out_ref[:, lanes] = (fit_scale * total).astype(jnp.bfloat16)
    core = lax.axis_index("rep") % 2
    action_half(rows, out_ref[...], mix_scale, 1 - core, width, ids(), send_ref)


def keep_kernel(mix_scale, width, ids, fitted_ref, *refs):
    core = lax.axis_index("rep") % 2
    action_half(refs[:-1], fitted_ref[...], mix_scale, core, width, ids(), refs[-1])


def action(fitted, early, late, ids, basis_rows, fit_scale, mix_scale):
    norb, cols = fitted[0].shape
    width = early[0].shape[1]
    blocks = basis_rows // width
    half = jax.ShapeDtypeStruct((blocks, width // 2, norb), jnp.float32)
    rows = list(early) + list(late)
    params = pltpu.CompilerParams(vmem_limit_bytes=VMEM_LIMIT)
    cost = pl.CostEstimate(
        flops=2 * blocks * width * cols * norb, bytes_accessed=2 * blocks * width * cols, transcendentals=0
    )
    send, columns = pl.pallas_call(
        functools.partial(
            send_kernel, fit_scale, mix_scale, min(512, cols), width, ids, len(early), len(late)
        ),
        out_shape=[half, jax.ShapeDtypeStruct((norb, cols), jnp.bfloat16)],
        in_specs=[pl.BlockSpec(memory_space=pltpu.VMEM)] * (len(fitted) + len(rows)),
        out_specs=[pl.BlockSpec(memory_space=pltpu.VMEM)] * 2,
        compiler_params=params,
        cost_estimate=cost,
    )(fitted[0], *rows, *fitted[1:])
    keep = pl.pallas_call(
        functools.partial(keep_kernel, mix_scale, width, ids),
        out_shape=half,
        in_specs=[pl.BlockSpec(memory_space=pltpu.VMEM)] * (1 + len(rows)),
        out_specs=pl.BlockSpec(memory_space=pltpu.VMEM),
        compiler_params=params,
        cost_estimate=cost,
    )(columns, *rows)
    return keep, send


def swapped(x, axis, k):
    return lax.ppermute(x, axis, [(i, i ^ k) for i in range(lax.axis_size(axis))])


def summed_blocks(blocks, axis):
    rows = blocks.shape[1]
    largest = jnp.max(jnp.abs(blocks), axis=1, keepdims=True)
    exponent = jnp.ceil(jnp.log2(jnp.maximum(largest, 1e-30))) - 14
    scaled = (blocks * jnp.exp2(-exponent)).astype(jnp.float16)
    tail = jnp.broadcast_to(exponent.astype(jnp.float16), (blocks.shape[0], 8, blocks.shape[2]))
    got = lax.all_to_all(jnp.concatenate([scaled, tail], axis=1), axis, 0, 0, tiled=True).astype(jnp.float32)
    return jnp.sum(got[:, :rows] * jnp.exp2(got[:, rows:rows + 1]), axis=0)


def per_device(orbitals, tiles, tile_block, tile_count):
    rep_size = lax.axis_size("rep")
    grid_size = lax.axis_size("grid")
    width = tiles.shape[3]
    depth, norb = orbitals.shape
    half = norb // 2
    cols = width * norb // grid_size
    basis_rows = depth * rep_size
    fit_scale = 1.0 / math.sqrt(basis_rows)
    mix_scale = 0.25 / math.sqrt(width * rep_size * norb)
    inside, block = load(tiles, tile_count, tile_block)
    per_part = half // grid_size
    if per_part == SUB and grid_size == 8 and rep_size == 4:
        parts = [orbitals] + [swapped(orbitals, "rep", k) for k in range(1, rep_size)]
        layers = grid_size // 2

        def target(at, move, sign=1):
            return (at // 2 + sign * move[0] + layers) % layers * 2 + (at % 2 ^ move[1])

        def ids(moves, sign):
            def blocks():
                me = lax.axis_index("grid")
                return [target(me, move, sign) for move in moves]

            return blocks

        def starts(moves):
            return lambda: [b * SUB for b in ids(moves, 1)()]

        def own_output(s, k):
            return s, 0, k

        def shapes(moves):
            return [(1, width, cols)] * len(moves)

        def moved(x, move):
            if move == (0, 0):
                return x
            return lax.ppermute(x, "grid", [(i, target(i, move)) for i in range(grid_size)])

        waves, late_moves = [[(1, 0)], [(0, 0), (0, 1), (3, 0), (2, 1)], [(2, 0), (1, 1), (3, 1)]], [(2, 0), (1, 1), (3, 1)]
        full, turned, made = contract_first(
            starts(waves[0]), None, [(2 * SUB, tiles.shape[4])], block, inside, parts, plain=True
        )
        sent = dict(zip(waves[0], made))
        for wave in waves[1:]:
            made = contract_next(starts(wave), own_output, shapes(wave), turned, inside, made[0])
            sent.update(zip(wave, made))
        received = {move: moved(sent[move], move) for move in sent}
        received[waves[0][0]] = arranged(received[waves[0][0]], width)
        early_moves = [move for move in received if move not in late_moves]
        early, late = [received[move] for move in early_moves], [received[move] for move in late_moves]
        early_ids, late_ids, all_ids = ids(early_moves, -1), ids(late_moves, -1), ids(early_moves + late_moves, -1)
    else:
        def place(s, k):
            part, col = divmod(s * SUB + k, per_part)
            return 0, part, col

        parts = [lax.all_gather(orbitals, "rep", axis=0, tiled=True)]
        full, _, (sent,) = contract_first(
            lambda: list(range(0, half, SUB)), place, [(grid_size, width, cols)], block, inside, parts
        )
        early, late = [lax.all_to_all(sent, "grid", 0, 0, tiled=True)], []

        def early_ids():
            return list(range(grid_size))

        late_ids, all_ids = None, early_ids
    fitted = fit(full, early, len(late), early_ids, late_ids)
    part_keep, part_send = action(fitted, early, late, all_ids, basis_rows, fit_scale, mix_scale)
    pair = part_keep + swapped(part_send, "rep", 1)
    mine = summed_blocks(pair, "grid")
    if rep_size == 4:
        other, across = swapped(mine, "rep", 2), swapped(mine, "rep", 3)
        beside = swapped(mine, "rep", 1)
        own, theirs = mine + other, beside + across
        upper = lax.axis_index("rep") % 2 == 1
        return jnp.concatenate([jnp.where(upper, theirs, own), jnp.where(upper, own, theirs)], axis=0)
    every = lax.all_gather(mine, "rep", axis=0, tiled=False)
    return jnp.sum(every.reshape(rep_size // 2, 2, width // 2, norb), axis=0).reshape(width, norb)


def solution(mesh):
    in_specs = (
        P("rep", None),
        P("rep", "grid", None, None, None),
        P("rep", "grid", None),
        P("rep", "grid"),
    )
    return jax.shard_map(
        per_device, mesh=mesh, in_specs=in_specs, out_specs=P("grid", None), check_vma=False
    )
```

```python
import functools
import math

import jax
import jax.numpy as jnp
from jax import lax
from jax.experimental import pallas as pl
from jax.experimental.pallas import tpu as pltpu
from jax.sharding import PartitionSpec as P

LANES = 128
SUB = 16
VMEM_LIMIT = 24 * 1024 * 1024


def load_kernel(count_ref, block_hbm, tiles_hbm, out_ref, live_ref, block, sems, block_sem):
    chunks = sems.shape[0]
    step = out_ref.shape[2] // chunks
    copies = [
        pltpu.make_async_copy(
            tiles_hbm.at[0, 0, :, :, pl.ds(at * step, step)], out_ref.at[:, :, pl.ds(at * step, step)], sems.at[at]
        )
        for at in range(chunks)
    ]
    block_copy = pltpu.make_async_copy(block_hbm, block, block_sem.at[0])
    block_copy.start()
    for each in copies:
        each.start()
    block_copy.wait()
    slot = lax.broadcasted_iota(jnp.int32, live_ref.shape, 1)
    live_ref[...] = jnp.where(slot < count_ref[0, 0], block[0], -1)
    for each in copies:
        each.wait()


def in_hbm(x):
    return pltpu.with_memory_space_constraint(x, pltpu.HBM)


def load(tiles, count, block):
    return pl.pallas_call(
        load_kernel,
        out_shape=[
            jax.ShapeDtypeStruct(tiles.shape[2:], tiles.dtype),
            jax.ShapeDtypeStruct(block.shape[1:], block.dtype),
        ],
        in_specs=[
            pl.BlockSpec(memory_space=pltpu.SMEM),
            pl.BlockSpec(memory_space=pltpu.HBM),
            pl.BlockSpec(memory_space=pltpu.HBM),
        ],
        out_specs=[pl.BlockSpec(memory_space=pltpu.VMEM)] * 2,
        scratch_shapes=[
            pltpu.VMEM(block.shape, block.dtype),
            pltpu.SemaphoreType.DMA((4,)),
            pltpu.SemaphoreType.DMA((1,)),
        ],
        compiler_params=pltpu.CompilerParams(vmem_limit_bytes=VMEM_LIMIT),
        cost_estimate=pl.CostEstimate(flops=0, bytes_accessed=2 * math.prod(tiles.shape), transcendentals=0),
    )(count, in_hbm(block), in_hbm(tiles))


def products(turned_ref, tiles_ref, group_starts):
    slots, width, extent = tiles_ref.shape
    half = turned_ref.shape[0] // 2
    step = SUB * width
    lhs = jnp.concatenate(
        [
            turned_ref[pl.ds(pl.multiple_of(first + at, SUB), SUB), :]
            for first in (0, half)
            for at in group_starts
        ],
        axis=0,
    )
    for at in range(extent // step):
        rhs = tiles_ref[:, :, at * step:(at + 1) * step].reshape(slots * width, step)
        yield at, jnp.dot(lhs, rhs, preferred_element_type=jnp.float32)


def arrange(chunks, groups, width, place, outs):
    row_at = lax.broadcasted_iota(jnp.int32, (SUB * SUB, SUB * SUB), 0)
    col_at = lax.broadcasted_iota(jnp.int32, (SUB * SUB, SUB * SUB), 1)
    bits = SUB.bit_length() - 1
    swap = (col_at == ((row_at & (SUB - 1)) << bits) + (row_at >> bits)).astype(jnp.bfloat16)
    low = lax.broadcasted_iota(jnp.int32, (SUB, LANES), 1) < width
    sides = []
    for at, acc in chunks:
        for s in range(groups):
            per_mu = []
            for q in range(acc.shape[1] // LANES):
                a = acc[s * SUB:(s + 1) * SUB, q * LANES:(q + 1) * LANES]
                b = acc[(groups + s) * SUB:(groups + s + 1) * SUB, q * LANES:(q + 1) * LANES]
                per_mu.append(jnp.where(low, a, pltpu.roll(b, width, 1)).astype(jnp.bfloat16))
                per_mu.append(jnp.where(low, pltpu.roll(a, width, 1), b).astype(jnp.bfloat16))
            sides.append((at, s, jnp.concatenate(per_mu, axis=0)))
    moved = jnp.dot(
        swap, jnp.concatenate([side for _, _, side in sides], axis=1), preferred_element_type=jnp.float32
    ).astype(jnp.bfloat16)
    for n, (at, s, _) in enumerate(sides):
        for k in range(SUB):
            which, part, col = place(s, k)
            outs[which][part, at * SUB:(at + 1) * SUB, col * LANES:(col + 1) * LANES] = moved[
                k * SUB:(k + 1) * SUB, n * LANES:(n + 1) * LANES
            ]


def multiply(turned_ref, tiles_ref, group_starts, place, outs):
    chunks = list(products(turned_ref, tiles_ref, group_starts))
    arrange(chunks, len(group_starts), tiles_ref.shape[1], place, outs)


def arrange_kernel(width, rows_ref, out_ref):
    step = SUB * width
    chunks = [
        (at, rows_ref[:, at * step:(at + 1) * step].astype(jnp.float32)) for at in range(rows_ref.shape[1] // step)
    ]
    arrange(chunks, 1, width, lambda s, k: (0, 0, k), [out_ref])


def arranged(rows, width):
    made = rows.shape[0] * rows.shape[1] // width
    return pl.pallas_call(
        functools.partial(arrange_kernel, width),
        out_shape=jax.ShapeDtypeStruct((1, width, made), rows.dtype),
        in_specs=[pl.BlockSpec(memory_space=pltpu.VMEM)],
        out_specs=pl.BlockSpec(memory_space=pltpu.VMEM),
        compiler_params=pltpu.CompilerParams(vmem_limit_bytes=VMEM_LIMIT),
        cost_estimate=pl.CostEstimate(
            flops=2 * SUB * SUB * width * made, bytes_accessed=4 * width * made, transcendentals=0
        ),
    )(rows)


def first_kernel(group_starts, place, n_parts, plain, block_ref, tiles_ref, *refs):
    parts, (full_ref, turned_ref, *outs), picked = refs[:n_parts], refs[n_parts:-1], refs[-1]
    slots, width, _ = tiles_ref.shape
    depth = parts[0].shape[0]
    me = lax.axis_index("rep") if n_parts > 1 else 0
    for k in range(n_parts):
        full_ref[pl.ds(pl.multiple_of((me ^ k) * depth, depth), depth), :] = parts[k][...]
    for t in range(slots):
        row = pl.multiple_of(jnp.maximum(block_ref[0, t], 0) * width, width)
        rows = full_ref[pl.ds(row, width), :]
        picked[t * width:(t + 1) * width, :] = jnp.where(block_ref[0, t] >= 0, rows, jnp.zeros_like(rows))
    turned_ref[...] = picked[...].T
    if plain:
        for at, acc in products(turned_ref, tiles_ref, group_starts()):
            step = acc.shape[1]
            outs[0][:, at * step:(at + 1) * step] = acc.astype(jnp.bfloat16)
    else:
        multiply(turned_ref, tiles_ref, group_starts(), place, outs)


def next_kernel(group_starts, place, turned_ref, tiles_ref, skipped, *outs):
    multiply(turned_ref, tiles_ref, group_starts(), place, outs)


def contract_cost(tiles, norb, out_shapes):
    slots, width, extent = tiles.shape
    made = sum(math.prod(shape) for shape in out_shapes)
    return pl.CostEstimate(
        flops=2 * slots * width * made, bytes_accessed=2 * slots * width * extent + 2 * made, transcendentals=0
    )


def contract_first(group_starts, place, out_shapes, block, tiles, parts, plain=False):
    slots, width, _ = tiles.shape
    depth, norb = parts[0].shape
    shapes = [(depth * len(parts), norb), (norb, slots * width)] + out_shapes
    full, turned, *made = pl.pallas_call(
        functools.partial(first_kernel, group_starts, place, len(parts), plain),
        out_shape=[jax.ShapeDtypeStruct(shape, jnp.bfloat16) for shape in shapes],
        in_specs=[pl.BlockSpec(memory_space=pltpu.VMEM)] * (2 + len(parts)),
        out_specs=[pl.BlockSpec(memory_space=pltpu.VMEM)] * len(shapes),
        scratch_shapes=[pltpu.VMEM((slots * width, norb), jnp.bfloat16)],
        compiler_params=pltpu.CompilerParams(vmem_limit_bytes=VMEM_LIMIT),
        cost_estimate=contract_cost(tiles, norb, out_shapes),
    )(block, tiles, *parts)
    return full, turned, made


def contract_next(group_starts, place, out_shapes, turned, tiles, after):
    return pl.pallas_call(
        functools.partial(next_kernel, group_starts, place),
        out_shape=[jax.ShapeDtypeStruct(shape, jnp.bfloat16) for shape in out_shapes],
        in_specs=[pl.BlockSpec(memory_space=pltpu.VMEM)] * 2 + [pl.BlockSpec(memory_space=pl.ANY)],
        out_specs=[pl.BlockSpec(memory_space=pltpu.VMEM)] * len(out_shapes),
        compiler_params=pltpu.CompilerParams(vmem_limit_bytes=VMEM_LIMIT),
        cost_estimate=contract_cost(tiles, turned.shape[0], out_shapes),
    )(turned, tiles, after)


def orbital_rows(orb_ref, width, ids):
    rows = [orb_ref[pl.ds(pl.multiple_of(b * width, width), width), :] for b in ids]
    return jnp.concatenate(rows, axis=0).T


def joined(refs, lanes=slice(None)):
    return jnp.concatenate([ref[:, :, lanes].reshape(-1, ref[:, :, lanes].shape[2]) for ref in refs], axis=0)


def fit_kernel(step, width, early_ids, late_ids, orb_ref, *refs):
    rows, (out_ref, *late_ref) = refs[:-1 - bool(late_ids)], refs[-1 - bool(late_ids):]
    turned = orbital_rows(orb_ref, width, early_ids())
    for at in range(out_ref.shape[1] // step):
        lanes = slice(at * step, (at + 1) * step)
        out_ref[:, lanes] = jnp.dot(turned, joined(rows, lanes), preferred_element_type=jnp.float32)
    if late_ids:
        late_ref[0][...] = orbital_rows(orb_ref, width, late_ids())


def fit(orbitals, early, n_late, early_ids, late_ids):
    width, cols = early[0].shape[1:]
    number = sum(each.shape[0] for each in early)
    norb = orbitals.shape[1]
    shapes = [jax.ShapeDtypeStruct((norb, cols), jnp.float32)]
    if n_late:
        shapes.append(jax.ShapeDtypeStruct((norb, n_late * width), jnp.bfloat16))
    return pl.pallas_call(
        functools.partial(fit_kernel, min(512, cols), width, early_ids, late_ids),
        out_shape=shapes,
        in_specs=[pl.BlockSpec(memory_space=pltpu.VMEM)] * (1 + len(early)),
        out_specs=[pl.BlockSpec(memory_space=pltpu.VMEM)] * len(shapes),
        compiler_params=pltpu.CompilerParams(vmem_limit_bytes=VMEM_LIMIT),
        cost_estimate=pl.CostEstimate(
            flops=2 * number * width * cols * norb,
            bytes_accessed=2 * number * width * cols + 4 * norb * cols,
            transcendentals=0,
        ),
    )(orbitals, *early)


def action_half(rows, fitted, mix_scale, half, width, ids, out_ref):
    offset = pl.multiple_of(half * (width // 2), width // 2)
    lhs = jnp.concatenate(
        [ref[b, pl.ds(offset, width // 2), :] for ref in rows for b in range(ref.shape[0])], axis=0
    )
    term = lax.dot_general(lhs, fitted, (((1,), (1,)), ((), ())), preferred_element_type=jnp.float32)
    term = (-mix_scale * term).reshape((-1,) + out_ref.shape[1:])
    for k, b in enumerate(ids):
        out_ref[b] = term[k]


def send_kernel(fit_scale, mix_scale, step, width, ids, n_early, n_late, fitted_ref, *refs):
    rows, late, (send_ref, out_ref) = refs[:n_early + n_late], refs[n_early:n_early + n_late], refs[-2:]
    cols = fitted_ref.shape[1]
    if late:
        turned = refs[n_early + n_late][...]
    for at in range(cols // step):
        lanes = slice(at * step, (at + 1) * step)
        total = fitted_ref[:, lanes]
        if late:
            total = total + jnp.dot(turned, joined(late, lanes), preferred_element_type=jnp.float32)
        out_ref[:, lanes] = (fit_scale * total).astype(jnp.bfloat16)
    core = lax.axis_index("rep") % 2
    action_half(rows, out_ref[...], mix_scale, 1 - core, width, ids(), send_ref)


def keep_kernel(mix_scale, width, ids, fitted_ref, *refs):
    core = lax.axis_index("rep") % 2
    action_half(refs[:-1], fitted_ref[...], mix_scale, core, width, ids(), refs[-1])


def action(fitted, early, late, ids, basis_rows, fit_scale, mix_scale):
    norb, cols = fitted[0].shape
    width = early[0].shape[1]
    blocks = basis_rows // width
    half = jax.ShapeDtypeStruct((blocks, width // 2, norb), jnp.float32)
    rows = list(early) + list(late)
    params = pltpu.CompilerParams(vmem_limit_bytes=VMEM_LIMIT)
    cost = pl.CostEstimate(
        flops=2 * blocks * width * cols * norb, bytes_accessed=2 * blocks * width * cols, transcendentals=0
    )
    send, columns = pl.pallas_call(
        functools.partial(
            send_kernel, fit_scale, mix_scale, cols, width, ids, len(early), len(late)
        ),
        out_shape=[half, jax.ShapeDtypeStruct((norb, cols), jnp.bfloat16)],
        in_specs=[pl.BlockSpec(memory_space=pltpu.VMEM)] * (len(fitted) + len(rows)),
        out_specs=[pl.BlockSpec(memory_space=pltpu.VMEM)] * 2,
        compiler_params=params,
        cost_estimate=cost,
    )(fitted[0], *rows, *fitted[1:])
    keep = pl.pallas_call(
        functools.partial(keep_kernel, mix_scale, width, ids),
        out_shape=half,
        in_specs=[pl.BlockSpec(memory_space=pltpu.VMEM)] * (1 + len(rows)),
        out_specs=pl.BlockSpec(memory_space=pltpu.VMEM),
        compiler_params=params,
        cost_estimate=cost,
    )(columns, *rows)
    return keep, send


def swapped(x, axis, k):
    return lax.ppermute(x, axis, [(i, i ^ k) for i in range(lax.axis_size(axis))])


def summed_blocks(blocks, axis):
    rows = blocks.shape[1]
    largest = jnp.max(jnp.abs(blocks), axis=1, keepdims=True)
    exponent = jnp.ceil(jnp.log2(jnp.maximum(largest, 1e-30))) - 14
    scaled = (blocks * jnp.exp2(-exponent)).astype(jnp.float16)
    tail = jnp.broadcast_to(exponent.astype(jnp.float16), (blocks.shape[0], 8, blocks.shape[2]))
    got = lax.all_to_all(jnp.concatenate([scaled, tail], axis=1), axis, 0, 0, tiled=True).astype(jnp.float32)
    return jnp.sum(got[:, :rows] * jnp.exp2(got[:, rows:rows + 1]), axis=0)


def per_device(orbitals, tiles, tile_block, tile_count):
    rep_size = lax.axis_size("rep")
    grid_size = lax.axis_size("grid")
    width = tiles.shape[3]
    depth, norb = orbitals.shape
    half = norb // 2
    cols = width * norb // grid_size
    basis_rows = depth * rep_size
    fit_scale = 1.0 / math.sqrt(basis_rows)
    mix_scale = 0.25 / math.sqrt(width * rep_size * norb)
    inside, block = load(tiles, tile_count, tile_block)
    per_part = half // grid_size
    if per_part == SUB and grid_size == 8 and rep_size == 4:
        parts = [orbitals] + [swapped(orbitals, "rep", k) for k in range(1, rep_size)]
        layers = grid_size // 2

        def target(at, move, sign=1):
            return (at // 2 + sign * move[0] + layers) % layers * 2 + (at % 2 ^ move[1])

        def ids(moves, sign):
            def blocks():
                me = lax.axis_index("grid")
                return [target(me, move, sign) for move in moves]

            return blocks

        def starts(moves):
            return lambda: [b * SUB for b in ids(moves, 1)()]

        def own_output(s, k):
            return s, 0, k

        def shapes(moves):
            return [(1, width, cols)] * len(moves)

        def moved(x, move):
            if move == (0, 0):
                return x
            return lax.ppermute(x, "grid", [(i, target(i, move)) for i in range(grid_size)])

        waves, late_moves = [[(1, 0)], [(0, 0), (3, 0), (2, 0)], [(2, 1), (3, 1), (1, 1), (0, 1)]], [(2, 1), (3, 1), (1, 1), (0, 1)]
        full, turned, made = contract_first(
            starts(waves[0]), None, [(2 * SUB, tiles.shape[4])], block, inside, parts, plain=True
        )
        sent = dict(zip(waves[0], made))
        for wave in waves[1:]:
            made = contract_next(starts(wave), own_output, shapes(wave), turned, inside, made[0])
            sent.update(zip(wave, made))
        received = {move: moved(sent[move], move) for move in sent}
        received[waves[0][0]] = arranged(received[waves[0][0]], width)
        early_moves = [move for move in received if move not in late_moves]
        early, late = [received[move] for move in early_moves], [received[move] for move in late_moves]
        early_ids, late_ids, all_ids = ids(early_moves, -1), ids(late_moves, -1), ids(early_moves + late_moves, -1)
    else:
        def place(s, k):
            part, col = divmod(s * SUB + k, per_part)
            return 0, part, col

        parts = [lax.all_gather(orbitals, "rep", axis=0, tiled=True)]
        full, _, (sent,) = contract_first(
            lambda: list(range(0, half, SUB)), place, [(grid_size, width, cols)], block, inside, parts
        )
        early, late = [lax.all_to_all(sent, "grid", 0, 0, tiled=True)], []

        def early_ids():
            return list(range(grid_size))

        late_ids, all_ids = None, early_ids
    fitted = fit(full, early, len(late), early_ids, late_ids)
    part_keep, part_send = action(fitted, early, late, all_ids, basis_rows, fit_scale, mix_scale)
    pair = part_keep + swapped(part_send, "rep", 1)
    mine = summed_blocks(pair, "grid")
    if rep_size == 4:
        other, across = swapped(mine, "rep", 2), swapped(mine, "rep", 3)
        beside = swapped(mine, "rep", 1)
        own, theirs = mine + other, beside + across
        upper = lax.axis_index("rep") % 2 == 1
        return jnp.concatenate([jnp.where(upper, theirs, own), jnp.where(upper, own, theirs)], axis=0)
    every = lax.all_gather(mine, "rep", axis=0, tiled=False)
    return jnp.sum(every.reshape(rep_size // 2, 2, width // 2, norb), axis=0).reshape(width, norb)


def solution(mesh):
    in_specs = (
        P("rep", None),
        P("rep", "grid", None, None, None),
        P("rep", "grid", None),
        P("rep", "grid"),
    )
    return jax.shard_map(
        per_device, mesh=mesh, in_specs=in_specs, out_specs=P("grid", None), check_vma=False
    )
```
